32 devices in a mesh: groups: 2 (over y), expert: 4 (over z), tensor: 2 (over x), dp: 2 (over core).
Axes of the slice: x: 2, y: 2, z: 4, core: 2. Of those that a mesh axis runs over, the one named last changes fastest.
Arguments:
- activations: bfloat16 [512, 2048], P(('groups', 'expert', 'dp'), 'tensor'), parts along dimension 0, may hold values from -6 to 6
- out_grad: bfloat16 [512, 2048], P(('groups', 'expert', 'dp'), 'tensor'), parts along dimension 0, may hold values from -1.5 to 1.5
- expert_ids: int32 [512, 8], P(('groups', 'expert', 'dp')), parts along dimension 0, may hold values from 0 to 31, all different within a row; in each aligned block of 32 rows (0 to 31, 32 to 63, ...) at most 16 rows name the same one
- gate_probs: bfloat16 [512, 8], P(('groups', 'expert', 'dp')), parts along dimension 0, may hold values from 0.049804688 to 0.5
- w_gate: bfloat16 [32, 2048, 768], P('expert', None, 'tensor'), may hold values from -0.125 to 0.125
- w_up: bfloat16 [32, 2048, 768], P('expert', None, 'tensor'), may hold values from -0.125 to 0.125
- w_down: bfloat16 [32, 768, 2048], P('expert', 'tensor'), may hold values from -0.21875 to 0.21875
Outputs:
- grad_activations: bfloat16 [512, 2048], P(('groups', 'expert', 'dp'), 'tensor'), parts along dimension 0
- grad_probs: float32 [512, 8], P(('groups', 'expert', 'dp')), parts along dimension 0
- grad_gate: bfloat16 [64, 2048, 768], P(('groups', 'expert'), None, 'tensor'), parts along dimension 0
- grad_up: bfloat16 [64, 2048, 768], P(('groups', 'expert'), None, 'tensor'), parts along dimension 0
- grad_down: bfloat16 [64, 768, 2048], P(('groups', 'expert'), 'tensor'), parts along dimension 0
The draws below stay inside these ranges and needn't reach their ends.
There are 2 independent parts, one for each index of `groups`. The reference program is written for one: setup_inputs(seed, part) draws one part's arguments, and reference() takes and returns one part's arrays. A program takes and returns all parts, laid end to end along the dimension named above; an argument that names none is the same for every part. Nothing has to cross between parts.
Inputs may be any that keep to these rules, and one draw needn't show every extreme that they name: `expert_ids`: among the 8 entries of a row, no expert appears twice. Among the 32 rows of one device, no expert appears in more than 16 rows, and in every draw some expert appears in exactly 16 of them.
All inputs are finite; a program needn't handle non-finite values.
Results may differ from the reference program's by a relative error of at most 0.009.
Values may be sent and summed in bfloat16 or wider, within the bound.
No kernel may reach another device: no remote copies, remote signals or barrier semaphores. Data moves between devices by JAX's collectives and lax.ppermute only.
A program may use at most 256 MiB of HBM per device.

```python
import math
import jax
import jax.numpy as jnp
import numpy as np
from jax import lax

D = 2048
FF = 768
EXPERTS = 32
TOP = 8
TOK_DEV = 32
CAP = 16
TOKENS = 256
N_EXPERT = 4
N_TENSOR = 2
N_DP = 2


def level_of(rng, extent, shards, smallest, high):
    loudness, own = 1.0, jax.random.fold_in(rng, 6)
    for dim, blocks in shards:
        steps = jnp.exp(jax.random.uniform(jax.random.fold_in(own, dim), (blocks,), jnp.float32, smallest / len(shards), high / len(shards)))
        loudness = loudness * jnp.repeat(steps, extent[dim] // blocks).reshape([-1 if axis == dim else 1 for axis in range(len(extent))])
    return loudness


def routed_block(own_key, own, number, rows, amount, top, reach, skew):
    order = jax.random.permutation(own_key, amount)
    crowded, ordinary = load_shares(amount, rows * top, reach, skew, True), load_shares(amount, rows * top, reach, skew, False)
    places = jnp.arange(amount)

    def named(sizes, offset_by):
        used = int((sizes > 0).sum())
        fixed = max(1, used // 4)
        passed = fixed + (places - fixed + offset_by * (used - fixed)) % max(1, amount - fixed)
        return jnp.zeros((amount,), jnp.int32).at[order[jnp.where(places < fixed, places, passed)]].set(jnp.asarray(sizes, jnp.int32))

    sizes = jnp.where(number % 4 == 0, named(crowded, number // 4), named(ordinary, number - number // 4 - 1))
    mixed = jax.random.permutation(jax.random.fold_in(own, 3), amount)
    giver, receiver = mixed[0:amount // 2 * 2:2], mixed[1:amount // 2 * 2:2]
    room = jnp.minimum(sizes[giver] - 1, reach - sizes[receiver]) // 2
    room = jnp.where((giver == order[0]) | (receiver == order[0]) | (sizes[receiver] == 0), 0, jnp.maximum(room, 0))
    passed = jax.random.randint(jax.random.fold_in(own, 4), (amount // 2,), 0, 1 << 20) % (room + 1)
    sizes = sizes.at[giver].add(-passed).at[receiver].add(passed)
    items = jnp.searchsorted(jnp.cumsum(sizes), jnp.arange(rows * top), side="right").astype(jnp.int32)
    table = items.reshape(top, rows).T
    table = table[jax.random.permutation(jax.random.fold_in(own, 1), rows)]
    offset_by = jax.random.randint(jax.random.fold_in(own, 2), (rows, 1), 0, top)
    return jnp.take_along_axis(table, (jnp.arange(top)[None, :] + offset_by) % top, axis=1)


def load_shares(number_of, total, bound, lean, full):
    loads = [(1 << 20) // math.isqrt(rank ** lean) + 1 for rank in range(1, number_of + 1)]
    largest = bound if full else min(bound, max(-(-total // number_of), total * loads[0] // sum(loads)))
    least = 1 if total - largest >= number_of - 1 else 0
    given, surplus = [largest] + [least] * (number_of - 1), total - largest - least * (number_of - 1)
    while surplus > 0:
        candidates = [i for i in range(1, number_of) if given[i] < largest] or [i for i in range(1, number_of) if given[i] < bound]
        whole, left = sum([loads[i] for i in candidates]), surplus
        for i in candidates:
            extra = min(bound - given[i], max(1, left * loads[i] // whole), surplus)
            given[i] = given[i] + extra
            surplus = surplus - extra
    return np.array(given)


def centred(rng, shape, scale, reach, shards=(), kind=jnp.bfloat16):
    array = scale * jax.random.normal(rng, shape, jnp.float32)
    if shards:
        array = array * level_of(rng, shape, shards, -0.22, 0.18)
    return jnp.clip(array, -reach, reach).astype(kind)


def setup_inputs(seed: int = 0, part: int = 0) -> dict:
    key_of = jax.random.split(jax.random.key(seed), 8)
    part_splits = jax.random.split(jax.random.fold_in(key_of[7], part), 8)
    activations = centred(part_splits[0], (TOKENS, D), 1.0, 6.0, ((0, 8), (1, 2)))
    out_grad = centred(part_splits[1], (TOKENS, D), 0.25, 1.5, ((0, 8), (1, 2)))
    expert_ids_keys = jax.random.split(jax.random.fold_in(part_splits[2], 1), TOKENS // TOK_DEV)
    expert_ids_turns = jax.random.permutation(jax.random.fold_in(part_splits[2], 3), TOKENS // TOK_DEV)
    expert_ids = jax.vmap(lambda own, number: routed_block(jax.random.fold_in(part_splits[2], 2), own, number, TOK_DEV, EXPERTS, TOP, CAP, 1))(expert_ids_keys, expert_ids_turns).reshape((TOKENS, TOP))
    gate_probs = jnp.clip(jnp.exp(math.log(0.5) - 2.306499 * jax.random.uniform(part_splits[3], (TOKENS, TOP), jnp.float32) ** level_of(part_splits[3], (TOKENS, TOP), ((0, 8),), -0.2, 0.2)), 0.049804688, 0.5).astype(jnp.bfloat16)
    w_gate = centred(key_of[4], (EXPERTS, D, FF), D ** -0.5, 0.125, ((0, 4), (2, 2)))
    w_up = centred(key_of[5], (EXPERTS, D, FF), D ** -0.5, 0.125, ((0, 4), (2, 2)))
    w_down = centred(key_of[6], (EXPERTS, FF, D), FF ** -0.5, 0.21875, ((0, 4), (1, 2)))
    return dict(activations=activations, out_grad=out_grad, expert_ids=expert_ids, gate_probs=gate_probs, w_gate=w_gate, w_up=w_up, w_down=w_down)


def round_half(values):
    rounded = lax.optimization_barrier(values.astype(jnp.bfloat16))
    return rounded.astype(jnp.float32)


def reference(activations, out_grad, expert_ids, gate_probs, w_gate, w_up, w_down):
    flat_ids = expert_ids.reshape(-1)
    pair_count = TOKENS * TOP
    pair_token = jnp.arange(pair_count, dtype=jnp.int32) // TOP
    pair_half = (pair_token // TOK_DEV) % N_DP
    pair_probs = gate_probs.reshape(-1).astype(jnp.float32)
    row_limit = N_EXPERT * CAP
    slice_width = FF // N_TENSOR

    def step(carry, inputs):
        grad_acc, prob_acc = carry
        expert, gate_w, up_w, down_w = inputs
        gate_sum = jnp.zeros((D, FF), jnp.float32)
        up_sum = jnp.zeros((D, FF), jnp.float32)
        down_sum = jnp.zeros((FF, D), jnp.float32)
        gate_split = gate_w.astype(jnp.float32).reshape(D, N_TENSOR, slice_width)
        up_split = up_w.astype(jnp.float32).reshape(D, N_TENSOR, slice_width)
        for half in range(N_DP):
            selected = (flat_ids == expert) & (pair_half == half)
            row_index = jnp.nonzero(selected, size=row_limit, fill_value=0)[0].astype(jnp.int32)
            is_valid = jnp.arange(row_limit, dtype=jnp.int32) < jnp.sum(selected.astype(jnp.int32))
            token_index = pair_token[row_index]
            rows_in = activations[token_index]
            grads_in = out_grad[token_index]
            row_probs = jnp.where(is_valid, pair_probs[row_index], 0.0)[:, None]
            gate_pre = jnp.dot(rows_in, gate_w, preferred_element_type=jnp.float32)
            up_pre = jnp.dot(rows_in, up_w, preferred_element_type=jnp.float32)
            hidden_grad = jnp.dot(grads_in, down_w.T, preferred_element_type=jnp.float32)
            sigma = jax.nn.sigmoid(gate_pre)
            activated = gate_pre * sigma
            hidden = activated * up_pre
            inner = round_half(jnp.sum((hidden * hidden_grad).reshape(row_limit, N_TENSOR, slice_width), axis=2))
            inner = jnp.sum(inner, axis=1)
            weighted = (row_probs * hidden).astype(jnp.bfloat16)
            scaled = row_probs * hidden_grad
            gate_grad = (scaled * up_pre * sigma * (1.0 + gate_pre * (1.0 - sigma))).astype(jnp.bfloat16)
            up_grad = (scaled * activated).astype(jnp.bfloat16)
            gate_slices = gate_grad.astype(jnp.float32).reshape(row_limit, N_TENSOR, slice_width)
            up_slices = up_grad.astype(jnp.float32).reshape(row_limit, N_TENSOR, slice_width)
            row_slices = jnp.einsum("rtf,dtf->rtd", gate_slices, gate_split) + jnp.einsum("rtf,dtf->rtd", up_slices, up_split)
            row_total = jnp.sum(round_half(row_slices), axis=1)
            grad_acc = grad_acc.at[token_index].add(jnp.where(is_valid[:, None], row_total, 0.0))
            prob_acc = prob_acc.at[row_index].add(jnp.where(is_valid, inner, 0.0))
            gate_sum = gate_sum + round_half(jnp.dot(rows_in.T, gate_grad, preferred_element_type=jnp.float32))
            up_sum = up_sum + round_half(jnp.dot(rows_in.T, up_grad, preferred_element_type=jnp.float32))
            down_sum = down_sum + round_half(jnp.dot(weighted.T, grads_in, preferred_element_type=jnp.float32))
        outputs = (gate_sum.astype(jnp.bfloat16), up_sum.astype(jnp.bfloat16), down_sum.astype(jnp.bfloat16))
        return (grad_acc, prob_acc), outputs

    start = (jnp.zeros((TOKENS, D), jnp.float32), jnp.zeros((pair_count,), jnp.float32))
    expert_index = jnp.arange(EXPERTS, dtype=jnp.int32)
    (grad_acc, prob_acc), (grad_gate, grad_up, grad_down) = lax.scan(step, start, (expert_index, w_gate, w_up, w_down))
    return grad_acc.astype(jnp.bfloat16), prob_acc.reshape(TOKENS, TOP), grad_gate, grad_up, grad_down
```

```python
import functools

import jax
import jax.numpy as jnp
from jax import lax
from jax.experimental import pallas as pl
from jax.experimental.pallas import tpu as pltpu
from jax.sharding import PartitionSpec as P

VMEM_BYTES = 56 * 1024 * 1024
CAP = 16
META = 128
NT = (((1,), (1,)), ((), ()))


def forward_kernel(places, parts, top, own, scalars, *refs):
    shards = refs[: len(places)]
    wg_ref, wu_ref, wd_ref = refs[len(places) : len(places) + 3]
    outs = refs[len(places) + 3 :]
    own_ref, other_ref, grads_ref, weighted_ref, xt_ref, og_ref, x_ref, meta_ref, acc_ref, inner_ref = outs
    step = pl.program_id(0)
    tensor, dp = scalars[1], scalars[2]
    n_tensor, n_dp = parts
    wide = x_ref.shape[1] // n_tensor
    tokens = x_ref.shape[0]
    share = tokens // n_dp

    @pl.when(step == 0)
    def _():
        for shard, (row, side, half) in zip(shards, places):
            rows = shard.shape[0]
            at = pl.ds(pl.multiple_of(lax.rem(dp + half, n_dp) * share + row, rows), rows)
            columns = pl.ds(pl.multiple_of(lax.rem(tensor + side, n_tensor) * wide, wide), wide)
            x_ref[at, columns] = shard[:, :wide]
            og_ref[at, columns] = shard[:, wide : 2 * wide]
            if side == 0:
                meta_ref[at, :] = shard[:, 2 * wide :].astype(jnp.float32)
        xt_ref[...] = x_ref[...].T
        inner_ref[...] = jnp.zeros_like(inner_ref)

    rows, grads = x_ref[...], og_ref[...]
    gate_pre = jnp.dot(rows, wg_ref[0], preferred_element_type=jnp.float32)
    up_pre = jnp.dot(rows, wu_ref[0], preferred_element_type=jnp.float32)
    hidden_grad = lax.dot_general(grads, wd_ref[0], NT, preferred_element_type=jnp.float32)
    expert = scalars[3] + step
    meta = meta_ref[...]
    hit = meta[:, :top] == expert.astype(jnp.float32)
    prob = jnp.sum(jnp.where(hit, meta[:, top : 2 * top], 0.0), axis=1, keepdims=True)
    sigma = jax.nn.sigmoid(gate_pre)
    activated = gate_pre * sigma
    hidden = activated * up_pre
    inner = jnp.sum(hidden * hidden_grad, axis=1, keepdims=True)
    lane = lax.broadcasted_iota(jnp.int32, inner_ref.shape, 1)
    inner_ref[...] = jnp.where(lane == expert, inner, inner_ref[...])
    scaled = prob * hidden_grad
    gate_grad = (scaled * up_pre * sigma * (1.0 + gate_pre * (1.0 - sigma))).astype(jnp.bfloat16)
    up_grad = (scaled * activated).astype(jnp.bfloat16)
    grads_ref[0, 0] = gate_grad
    grads_ref[0, 1] = up_grad
    weighted_ref[0] = (prob * hidden).T.astype(jnp.bfloat16)
    row_part = lax.dot_general(gate_grad, wg_ref[0], NT, preferred_element_type=jnp.float32)
    row_part = row_part + lax.dot_general(up_grad, wu_ref[0], NT, preferred_element_type=jnp.float32)

    @pl.when(step == 0)
    def _():
        acc_ref[...] = row_part

    @pl.when(step > 0)
    def _():
        acc_ref[...] += row_part

    @pl.when(step == own - 1)
    def _():
        for half, target in ((0, own_ref), (1, other_ref)):
            if target is None:
                continue
            at = pl.ds(pl.multiple_of(lax.rem(dp + half, n_dp) * share, share), share)
            for side in range(n_tensor):
                columns = pl.ds(pl.multiple_of(lax.rem(tensor + side, n_tensor) * wide, wide), wide)
                target[side, :, :wide] = acc_ref[at, columns].astype(target.dtype)
                target[side, :, wide:] = inner_ref[at, :].astype(jnp.bfloat16).astype(target.dtype)


def forward(shards, places, scalars, w_gate, w_up, w_down, own, tokens, parts, top):
    n_tensor, n_dp = parts
    _, d, ff = w_gate.shape
    share, wide = tokens // n_dp, d // n_tensor
    whole = lambda shape: pl.BlockSpec(shape, lambda i, s: (0,) * len(shape))
    weight = lambda shape: pl.BlockSpec((1, *shape), lambda i, s: (s[0] + i, 0, 0))
    sums = (n_tensor, share, wide + META)
    return pl.pallas_call(
        functools.partial(forward_kernel, places, parts, top, own),
        grid_spec=pltpu.PrefetchScalarGridSpec(
            num_scalar_prefetch=1,
            grid=(own,),
            in_specs=[whole(s.shape) for s in shards] + [weight((d, ff)), weight((d, ff)), weight((ff, d))],
            out_specs=[
                whole(sums),
                whole(sums),
                pl.BlockSpec((1, 2, tokens, ff), lambda i, s: (i, 0, 0, 0)),
                pl.BlockSpec((1, ff, tokens), lambda i, s: (i, 0, 0)),
                whole((d, tokens)),
                whole((tokens, d)),
            ],
            scratch_shapes=[
                pltpu.VMEM((tokens, d), jnp.bfloat16),
                pltpu.VMEM((tokens, META), jnp.float32),
                pltpu.VMEM((tokens, d), jnp.float32),
                pltpu.VMEM((tokens, META), jnp.float32),
            ],
        ),
        out_shape=[
            jax.ShapeDtypeStruct(sums, jnp.float32),
            jax.ShapeDtypeStruct(sums, jnp.bfloat16),
            jax.ShapeDtypeStruct((own, 2, tokens, ff), jnp.bfloat16),
            jax.ShapeDtypeStruct((own, ff, tokens), jnp.bfloat16),
            jax.ShapeDtypeStruct((d, tokens), jnp.bfloat16),
            jax.ShapeDtypeStruct((tokens, d), jnp.bfloat16),
        ],
        compiler_params=pltpu.CompilerParams(vmem_limit_bytes=VMEM_BYTES),
        cost_estimate=pl.CostEstimate(
            flops=10 * own * tokens * d * ff, bytes_accessed=6 * own * d * ff + 8 * tokens * d, transcendentals=0
        ),
        name="routed_forward",
    )(scalars, *shards, w_gate, w_up, w_down)


def weight_kernel(scalars, xt_ref, og_ref, grads_ref, weighted_ref, *refs):
    gate_ref, up_ref, down_ref = refs[-3:]
    xt = xt_ref[...]
    gate_ref[0] = jnp.dot(xt, grads_ref[0, 0], preferred_element_type=jnp.float32).astype(jnp.bfloat16)
    up_ref[0] = jnp.dot(xt, grads_ref[0, 1], preferred_element_type=jnp.float32).astype(jnp.bfloat16)
    down_ref[0] = jnp.dot(weighted_ref[0], og_ref[...], preferred_element_type=jnp.float32).astype(jnp.bfloat16)


def weight_grads(scalars, xt, og, grads, weighted, local_count, into=None):
    own, _, tokens, ff = grads.shape
    d = xt.shape[0]
    whole = lambda shape: pl.BlockSpec(shape, lambda i, s: (0,) * len(shape))
    out = lambda shape: pl.BlockSpec((1, *shape), lambda i, s: (s[0] + i, 0, 0))
    kept = [] if into is None else list(into)
    shapes = [(d, ff), (d, ff), (ff, d)]
    return pl.pallas_call(
        weight_kernel,
        grid_spec=pltpu.PrefetchScalarGridSpec(
            num_scalar_prefetch=1,
            grid=(own,),
            in_specs=[
                whole((d, tokens)),
                whole((tokens, d)),
                pl.BlockSpec((1, 2, tokens, ff), lambda i, s: (i, 0, 0, 0)),
                pl.BlockSpec((1, ff, tokens), lambda i, s: (i, 0, 0)),
            ]
            + [pl.BlockSpec(memory_space=pl.ANY)] * len(kept),
            out_specs=[out(s) for s in shapes],
        ),
        out_shape=[jax.ShapeDtypeStruct((local_count, *s), jnp.bfloat16) for s in shapes],
        input_output_aliases={5 + i: i for i in range(len(kept))},
        compiler_params=pltpu.CompilerParams(vmem_limit_bytes=VMEM_BYTES),
        cost_estimate=pl.CostEstimate(
            flops=6 * own * tokens * d * ff, bytes_accessed=6 * own * d * ff + 8 * tokens * d, transcendentals=0
        ),
        name="weight_grads",
    )(scalars, xt, og, grads, weighted, *kept)


def split_kernel(own_ref, got_ref, *out_refs):
    rows, sides = out_refs[0].shape[0], own_ref.shape[0]
    blocks = own_ref.shape[1] // rows
    for side in range(sides):
        for block in range(blocks):
            at = pl.ds(block * rows, rows)
            total = own_ref[side, at, :] + got_ref[side, at, :].astype(jnp.float32)
            out_refs[side * blocks + block][...] = total.astype(out_refs[0].dtype)


def finish_kernel(top, ids_ref, *refs):
    parts, (grad_ref, probs_ref) = refs[:-2], refs[-2:]
    total = parts[0][...].astype(jnp.float32)
    for part in parts[1:]:
        total = total + part[...].astype(jnp.float32)
    wide = grad_ref.shape[1]
    grad_ref[...] = total[:, :wide].astype(jnp.bfloat16)
    inner = total[:, wide:]
    ids = ids_ref[...]
    lane = lax.broadcasted_iota(jnp.int32, inner.shape, 1)
    for k in range(top):
        picked = jnp.where(lane == ids[:, k : k + 1], inner, 0.0)
        probs_ref[:, k : k + 1] = jnp.sum(picked, axis=1, keepdims=True)


def shift(x, axis, by):
    count = lax.axis_size(axis)
    return lax.ppermute(x, axis, [(i, (i + by) % count) for i in range(count)])


def shift_both(x, by, side):
    n_expert, n_tensor = lax.axis_size("expert"), lax.axis_size("tensor")
    pairs = [
        (e * n_tensor + t, (e + by) % n_expert * n_tensor + (t + side) % n_tensor)
        for e in range(n_expert)
        for t in range(n_tensor)
    ]
    return lax.ppermute(x, ("expert", "tensor"), pairs)


def general_body(activations, out_grad, expert_ids, gate_probs, w_gate, w_up, w_down):
    d = activations.shape[1] * lax.axis_size("tensor")
    expert_count = lax.axis_size("expert")
    local_count = w_gate.shape[0]
    experts = expert_count * local_count
    token_rows = expert_ids.shape[0]
    flat_ids = expert_ids.reshape(-1)
    onehot = (flat_ids[:, None] == jnp.arange(experts, dtype=jnp.int32)[None, :]).astype(jnp.int32)
    before = jnp.cumsum(onehot, axis=0) - onehot
    slot_index = jnp.sum(before * onehot, axis=1)
    position = (flat_ids * CAP + slot_index).reshape(token_rows, expert_ids.shape[1])
    lane_index = jnp.arange(experts * CAP, dtype=jnp.int32)
    matches = position[None, :, :] == lane_index[:, None, None]
    placing = jnp.sum(matches.astype(jnp.int32), axis=2).astype(jnp.bfloat16)
    send_probs = jnp.sum(jnp.where(matches, gate_probs.astype(jnp.float32)[None], 0.0), axis=(1, 2))
    send_probs = send_probs.astype(jnp.bfloat16).reshape(experts, CAP)
    full_rows, full_grads = (
        lax.all_gather(activations, "tensor", axis=1, tiled=True),
        lax.all_gather(out_grad, "tensor", axis=1, tiled=True),
    )
    send_rows = (
        jnp.dot(placing, full_rows, preferred_element_type=jnp.float32)
        .astype(jnp.bfloat16)
        .reshape(experts, CAP, d)
    )
    send_grads = (
        jnp.dot(placing, full_grads, preferred_element_type=jnp.float32)
        .astype(jnp.bfloat16)
        .reshape(experts, CAP, d)
    )
    got_rows, got_grads, got_probs = (
        lax.all_to_all(send_rows, "expert", split_axis=0, concat_axis=0, tiled=True),
        lax.all_to_all(send_grads, "expert", split_axis=0, concat_axis=0, tiled=True),
        lax.all_to_all(send_probs, "expert", split_axis=0, concat_axis=0, tiled=True),
    )
    rows_in = got_rows.reshape(expert_count, local_count, CAP, d)
    grads_in = got_grads.reshape(expert_count, local_count, CAP, d)
    row_probs = got_probs.reshape(expert_count, local_count, CAP, 1).astype(jnp.float32)
    gate_pre = jnp.einsum("slcd,ldf->slcf", rows_in, w_gate, preferred_element_type=jnp.float32)
    up_pre = jnp.einsum("slcd,ldf->slcf", rows_in, w_up, preferred_element_type=jnp.float32)
    hidden_grad = jnp.einsum("slcd,lfd->slcf", grads_in, w_down, preferred_element_type=jnp.float32)
    sigma = jax.nn.sigmoid(gate_pre)
    activated = gate_pre * sigma
    hidden = activated * up_pre
    inner_part = jnp.sum(hidden * hidden_grad, axis=3)
    weighted = (row_probs * hidden).astype(jnp.bfloat16)
    scaled = row_probs * hidden_grad
    gate_grad = (scaled * up_pre * sigma * (1.0 + gate_pre * (1.0 - sigma))).astype(jnp.bfloat16)
    up_grad = (scaled * activated).astype(jnp.bfloat16)
    row_part = jnp.einsum("slcf,ldf->slcd", gate_grad, w_gate, preferred_element_type=jnp.float32)
    row_part = row_part + jnp.einsum(
        "slcf,ldf->slcd", up_grad, w_up, preferred_element_type=jnp.float32
    )
    gate_total = jnp.einsum(
        "slcd,slcf->ldf", rows_in, gate_grad, preferred_element_type=jnp.float32
    )
    up_total = jnp.einsum("slcd,slcf->ldf", rows_in, up_grad, preferred_element_type=jnp.float32)
    down_total = jnp.einsum(
        "slcf,slcd->lfd", weighted, grads_in, preferred_element_type=jnp.float32
    )
    lanes = experts * CAP
    own_part = lax.psum_scatter(
        row_part.astype(jnp.bfloat16), "tensor", scatter_dimension=3, tiled=True
    ).astype(jnp.float32)
    inner_sum = lax.psum(inner_part.astype(jnp.bfloat16), "tensor").astype(jnp.float32)
    quarter = own_part.shape[3]
    returned_rows, returned_inner = (
        lax.all_to_all(
            own_part.reshape(experts, CAP, quarter).astype(jnp.bfloat16),
            "expert",
            split_axis=0,
            concat_axis=0,
            tiled=True,
        ).astype(jnp.float32),
        lax.all_to_all(
            inner_sum.reshape(experts, CAP).astype(jnp.bfloat16),
            "expert",
            split_axis=0,
            concat_axis=0,
            tiled=True,
        ).astype(jnp.float32),
    )
    placing_wide = jnp.sum(matches.astype(jnp.int32), axis=2).astype(jnp.float32)
    token_grad = lax.dot_general(
        placing_wide,
        returned_rows.reshape(lanes, quarter),
        (((0,), (0,)), ((), ())),
        precision=lax.Precision.HIGHEST,
        preferred_element_type=jnp.float32,
    )
    grad_probs = jnp.sum(
        jnp.where(matches, returned_inner.reshape(lanes)[:, None, None], 0.0), axis=0
    )
    gate_sum, up_sum, down_sum = (
        lax.psum(gate_total.astype(jnp.bfloat16), "dp").astype(jnp.float32),
        lax.psum(up_total.astype(jnp.bfloat16), "dp").astype(jnp.float32),
        lax.psum(down_total.astype(jnp.bfloat16), "dp").astype(jnp.float32),
    )
    return (
        token_grad.astype(jnp.bfloat16),
        grad_probs,
        gate_sum.astype(jnp.bfloat16),
        up_sum.astype(jnp.bfloat16),
        down_sum.astype(jnp.bfloat16),
    )


def body(activations, out_grad, expert_ids, gate_probs, w_gate, w_up, w_down):
    n_expert, n_tensor, n_dp = (lax.axis_size(a) for a in ("expert", "tensor", "dp"))
    local_count, d, ff = w_gate.shape
    rows, top = expert_ids.shape
    tokens = rows * n_expert * n_dp
    wide = d // n_tensor
    own = local_count // n_dp
    e, t, p = (lax.axis_index(a) for a in ("expert", "tensor", "dp"))
    first = p * own
    meta = jnp.concatenate([expert_ids.astype(jnp.bfloat16), gate_probs], axis=1)
    meta = jnp.pad(meta, ((0, 0), (0, META - 2 * top)))
    packed = jnp.concatenate([activations, out_grad, meta], axis=1)
    shards, places = [], []
    along = [packed] + [shift(packed, "expert", k) for k in range(1, n_expert)]
    for side in range(n_tensor):
        for k in range(n_expert):
            shards.append(along[k] if side == 0 else shift(along[k], "tensor", 1))
            places.append((k * rows, side, 0))
    for i in range(n_expert * n_tensor):
        shards.append(shift(shards[i], "dp", 1))
        places.append((*places[i][:2], 1))
    scalars = jnp.stack([first, t, p, e * local_count + first]).astype(jnp.int32)
    own_sum, other_sum, grads, weighted, xt, og = forward(
        shards, tuple(places), scalars, w_gate, w_up, w_down, own, tokens, (n_tensor, n_dp), top
    )
    from_other = shift(other_sum, "dp", 1)
    piece = jax.ShapeDtypeStruct((rows, wide + META), jnp.bfloat16)
    pieces = pl.pallas_call(
        split_kernel, out_shape=[piece] * (n_expert * n_tensor), name="add_and_split"
    )(own_sum, from_other)
    got_grads, got_weighted = shift(grads, "dp", 1), shift(weighted, "dp", 1)
    received = []
    for side in range(n_tensor):
        for k in range(n_expert):
            part = pieces[side * n_expert + k]
            received.append(part if side == k == 0 else shift_both(part, -k, side))
    outputs = weight_grads(scalars, xt, og, grads, weighted, local_count)
    other = jnp.stack([own - first, t]).astype(jnp.int32)
    outputs = weight_grads(other, xt, og, got_grads, got_weighted, local_count, outputs)
    grad, probs = pl.pallas_call(
        functools.partial(finish_kernel, top),
        out_shape=[jax.ShapeDtypeStruct((rows, wide), jnp.bfloat16), jax.ShapeDtypeStruct((rows, top), jnp.float32)],
        name="sum_of_parts",
    )(expert_ids, *received)
    return (grad, probs, *outputs)


def solution(mesh):
    in_specs = (
        P(("groups", "expert", "dp"), "tensor"),
        P(("groups", "expert", "dp"), "tensor"),
        P(("groups", "expert", "dp"), None),
        P(("groups", "expert", "dp"), None),
        P("expert", None, "tensor"),
        P("expert", None, "tensor"),
        P("expert", "tensor", None),
    )
    out_specs = (
        P(("groups", "expert", "dp"), "tensor"),
        P(("groups", "expert", "dp"), None),
        P(("groups", "expert"), None, "tensor"),
        P(("groups", "expert"), None, "tensor"),
        P(("groups", "expert"), "tensor", None),
    )
    sizes = dict(mesh.shape)
    compact = sizes["expert"] <= 4 and sizes["tensor"] == 2 and sizes["dp"] == 2
    return jax.shard_map(body if compact else general_body, mesh=mesh, in_specs=in_specs, out_specs=out_specs, check_vma=False)
```

```python
import functools

import jax
import jax.numpy as jnp
from jax import lax
from jax.experimental import pallas as pl
from jax.experimental.pallas import tpu as pltpu
from jax.sharding import PartitionSpec as P

CAP = 16
META = 128
MIB = 1024 * 1024
NT = (((1,), (1,)), ((), ()))
TN = (((0,), (0,)), ((), ()))
ANY = pl.BlockSpec(memory_space=pl.ANY)
SMEM = pl.BlockSpec(memory_space=pltpu.SMEM)
VMEM = pl.BlockSpec(memory_space=pltpu.VMEM)


def near(*arrays):
    return [pltpu.with_memory_space_constraint(x, pltpu.VMEM) for x in arrays]


def far(*arrays):
    return [pltpu.with_memory_space_constraint(x, pltpu.HBM) for x in arrays]


def load_kernel(own, first_ref, wg_ref, wu_ref, wd_ref, in_ref, out_ref, sem):
    ff = wd_ref.shape[1]
    copies = []
    for i in range(own):
        for j, source in enumerate((wg_ref, wu_ref)):
            target = in_ref.at[:, pl.ds((2 * i + j) * ff, ff)]
            copies.append(pltpu.make_async_copy(source.at[first_ref[0] + i], target, sem))
        copies.append(pltpu.make_async_copy(wd_ref.at[first_ref[0] + i], out_ref.at[pl.ds(i * ff, ff), :], sem))
    for copy in copies:
        copy.start()
    for copy in copies:
        copy.wait()


def load_weights(scalars, w_gate, w_up, w_down, own):
    _, d, ff = w_gate.shape
    return pl.pallas_call(
        functools.partial(load_kernel, own),
        in_specs=[SMEM, ANY, ANY, ANY],
        out_specs=[VMEM, VMEM],
        out_shape=[pltpu.VMEM((d, own * 2 * ff), jnp.bfloat16), pltpu.VMEM((own * ff, d), jnp.bfloat16)],
        scratch_shapes=[pltpu.SemaphoreType.DMA],
        compiler_params=pltpu.CompilerParams(vmem_limit_bytes=4 * MIB),
        cost_estimate=pl.CostEstimate(flops=0, bytes_accessed=6 * own * d * ff, transcendentals=0),
        name="load_weights",
    )(scalars, *far(w_gate, w_up, w_down))


def forward_kernel(places, n_tensor, top, own, scalars, *refs):
    count = len(places)
    shards, (w_in, w_out) = refs[:count], refs[count : count + 2]
    x_ref, og_ref, grads_ref, kept_ref, sent_ref, meta_ref = refs[count + 2 :]
    tensor = scalars[1]
    tokens, d = x_ref.shape
    wide, share = d // n_tensor, tokens // 2
    ff = w_out.shape[0] // own
    for shard, (row, side) in zip(shards, places):
        rows = shard.shape[0]
        columns = pl.ds(pl.multiple_of(lax.rem(tensor + side, n_tensor) * wide, wide), wide)
        x_ref[pl.ds(row, rows), columns] = shard[:, :wide]
        og_ref[pl.ds(row, rows), columns] = shard[:, wide : 2 * wide]
        if side == 0:
            meta_ref[pl.ds(row, rows), :] = shard[:, 2 * wide :].astype(jnp.float32)
    pre = jnp.dot(x_ref[...], w_in[...], preferred_element_type=jnp.float32)
    hidden_grads = lax.dot_general(og_ref[...], w_out[...], NT, preferred_element_type=jnp.float32)
    meta = meta_ref[...]
    lane = lax.broadcasted_iota(jnp.int32, meta.shape, 1)
    inners = jnp.zeros(meta.shape, jnp.float32)
    both = []
    for i in range(own):
        gate_pre, up_pre = pre[:, 2 * i * ff : (2 * i + 1) * ff], pre[:, (2 * i + 1) * ff : (2 * i + 2) * ff]
        hidden_grad = hidden_grads[:, i * ff : (i + 1) * ff]
        expert = scalars[2] + i
        hit = meta[:, :top] == expert.astype(jnp.float32)
        prob = jnp.sum(jnp.where(hit, meta[:, top : 2 * top], 0.0), axis=1, keepdims=True)
        sigma = jax.nn.sigmoid(gate_pre)
        activated = gate_pre * sigma
        hidden = activated * up_pre
        inner = jnp.sum(hidden * hidden_grad, axis=1, keepdims=True)
        inners = jnp.where(lane == expert, inner, inners)
        scaled = prob * hidden_grad
        gate_grad = (scaled * up_pre * sigma * (1.0 + gate_pre * (1.0 - sigma))).astype(jnp.bfloat16)
        up_grad = (scaled * activated).astype(jnp.bfloat16)
        grads_ref[i, :, :ff] = gate_grad
        grads_ref[i, :, ff : 2 * ff] = up_grad
        grads_ref[i, :, 2 * ff :] = (prob * hidden).astype(jnp.bfloat16)
        both += [gate_grad, up_grad]
    both = jnp.concatenate(both, axis=1)
    for side in range(n_tensor):
        at = pl.ds(pl.multiple_of(lax.rem(tensor + side, n_tensor) * wide, wide), wide)
        total = lax.dot_general(both, w_in[at, :], NT, preferred_element_type=jnp.float32)
        kept_ref[side, :, :wide] = total[:share]
        kept_ref[side, :, wide:] = inners[:share]
        sent_ref[side, :, :wide] = total[share:].astype(jnp.bfloat16)
        sent_ref[side, :, wide:] = inners[share:].astype(jnp.bfloat16)


def forward(shards, places, scalars, w_in, w_out, own, tokens, n_tensor, top):
    d, ff = w_out.shape[1], w_out.shape[0] // own
    sums = (n_tensor, tokens // 2, d // n_tensor + META)
    return pl.pallas_call(
        functools.partial(forward_kernel, places, n_tensor, top, own),
        in_specs=[SMEM] + [VMEM] * (len(shards) + 2),
        out_specs=[VMEM] * 5,
        out_shape=[
            pltpu.VMEM((tokens, d), jnp.bfloat16),
            pltpu.VMEM((tokens, d), jnp.bfloat16),
            pltpu.VMEM((own, tokens, 3 * ff), jnp.bfloat16),
            pltpu.VMEM(sums, jnp.float32),
            pltpu.VMEM(sums, jnp.bfloat16),
        ],
        scratch_shapes=[pltpu.VMEM((tokens, META), jnp.float32)],
        compiler_params=pltpu.CompilerParams(vmem_limit_bytes=20 * MIB),
        cost_estimate=pl.CostEstimate(
            flops=10 * own * tokens * d * ff, bytes_accessed=16 * tokens * d, transcendentals=0
        ),
        name="routed_forward",
    )(scalars, *near(*shards), w_in, w_out)


def weight_kernel(swap, scalars, x_ref, og_ref, grads_ref, *refs):
    gate_ref, up_ref, down_ref = refs[-3:]
    ff = gate_ref.shape[2]
    grads = grads_ref[0]
    if swap:
        half = grads.shape[0] // 2
        grads = jnp.concatenate([grads[half:], grads[:half]], axis=0)
    both = lax.dot_general(x_ref[...], grads[:, : 2 * ff], TN, preferred_element_type=jnp.float32)
    gate_ref[0] = both[:, :ff].astype(jnp.bfloat16)
    up_ref[0] = both[:, ff:].astype(jnp.bfloat16)
    down = lax.dot_general(grads[:, 2 * ff :], og_ref[...], TN, preferred_element_type=jnp.float32)
    down_ref[0] = down.astype(jnp.bfloat16)


def weight_grads(scalars, x, og, grads, local_count, into=None):
    own, tokens, ff = grads.shape[0], grads.shape[1], grads.shape[2] // 3
    d = x.shape[1]
    whole = pl.BlockSpec((tokens, d), lambda i, s: (0, 0))
    out = lambda shape: pl.BlockSpec((1, *shape), lambda i, s: (s[0] + i, 0, 0))
    kept = [] if into is None else list(into)
    shapes = [(d, ff), (d, ff), (ff, d)]
    return pl.pallas_call(
        functools.partial(weight_kernel, into is not None),
        grid_spec=pltpu.PrefetchScalarGridSpec(
            num_scalar_prefetch=1,
            grid=(own,),
            in_specs=[whole, whole, pl.BlockSpec((1, tokens, 3 * ff), lambda i, s: (i, 0, 0))] + [ANY] * len(kept),
            out_specs=[out(s) for s in shapes],
        ),
        out_shape=[jax.ShapeDtypeStruct((local_count, *s), jnp.bfloat16) for s in shapes],
        input_output_aliases={4 + i: i for i in range(len(kept))},
        compiler_params=pltpu.CompilerParams(vmem_limit_bytes=32 * MIB),
        cost_estimate=pl.CostEstimate(
            flops=6 * own * tokens * d * ff, bytes_accessed=6 * own * d * ff + 8 * tokens * d, transcendentals=0
        ),
        name="weight_grads",
    )(scalars, x, og, grads, *kept)


def dp_sum_kernel(kept_ref, got_ref, here_ref, there_ref):
    here_ref[...] = kept_ref[0] + got_ref[0].astype(jnp.float32)
    there_ref[...] = (kept_ref[1] + got_ref[1].astype(jnp.float32)).astype(jnp.bfloat16)


def tensor_sum_kernel(here_ref, got_ref, own_ref, *out_refs):
    rows = own_ref.shape[0]
    for block, target in enumerate((own_ref, *out_refs)):
        at = pl.ds(block * rows, rows)
        target[...] = (here_ref[at, :] + got_ref[at, :].astype(jnp.float32)).astype(target.dtype)


def finish_kernel(top, ids_ref, own_ref, *refs):
    parts, (grad_ref, probs_ref) = refs[:-2], refs[-2:]
    total = own_ref[...]
    for part in parts:
        total = total + part[...].astype(jnp.float32)
    wide = grad_ref.shape[1]
    grad_ref[...] = total[:, :wide].astype(jnp.bfloat16)
    inner = total[:, wide:]
    ids = ids_ref[...]
    lane = lax.broadcasted_iota(jnp.int32, inner.shape, 1)
    for k in range(top):
        picked = jnp.where(lane == ids[:, k : k + 1], inner, 0.0)
        probs_ref[:, k : k + 1] = jnp.sum(picked, axis=1, keepdims=True)


def shift(x, axis, by):
    count = lax.axis_size(axis)
    return lax.ppermute(x, axis, [(i, (i + by) % count) for i in range(count)])


def general_body(activations, out_grad, expert_ids, gate_probs, w_gate, w_up, w_down):
    d = activations.shape[1] * lax.axis_size("tensor")
    expert_count = lax.axis_size("expert")
    local_count = w_gate.shape[0]
    experts = expert_count * local_count
    token_rows = expert_ids.shape[0]
    flat_ids = expert_ids.reshape(-1)
    onehot = (flat_ids[:, None] == jnp.arange(experts, dtype=jnp.int32)[None, :]).astype(jnp.int32)
    before = jnp.cumsum(onehot, axis=0) - onehot
    slot_index = jnp.sum(before * onehot, axis=1)
    position = (flat_ids * CAP + slot_index).reshape(token_rows, expert_ids.shape[1])
    lane_index = jnp.arange(experts * CAP, dtype=jnp.int32)
    matches = position[None, :, :] == lane_index[:, None, None]
    placing = jnp.sum(matches.astype(jnp.int32), axis=2).astype(jnp.bfloat16)
    send_probs = jnp.sum(jnp.where(matches, gate_probs.astype(jnp.float32)[None], 0.0), axis=(1, 2))
    send_probs = send_probs.astype(jnp.bfloat16).reshape(experts, CAP)
    full_rows, full_grads = (
        lax.all_gather(activations, "tensor", axis=1, tiled=True),
        lax.all_gather(out_grad, "tensor", axis=1, tiled=True),
    )
    send_rows = (
        jnp.dot(placing, full_rows, preferred_element_type=jnp.float32)
        .astype(jnp.bfloat16)
        .reshape(experts, CAP, d)
    )
    send_grads = (
        jnp.dot(placing, full_grads, preferred_element_type=jnp.float32)
        .astype(jnp.bfloat16)
        .reshape(experts, CAP, d)
    )
    got_rows, got_grads, got_probs = (
        lax.all_to_all(send_rows, "expert", split_axis=0, concat_axis=0, tiled=True),
        lax.all_to_all(send_grads, "expert", split_axis=0, concat_axis=0, tiled=True),
        lax.all_to_all(send_probs, "expert", split_axis=0, concat_axis=0, tiled=True),
    )
    rows_in = got_rows.reshape(expert_count, local_count, CAP, d)
    grads_in = got_grads.reshape(expert_count, local_count, CAP, d)
    row_probs = got_probs.reshape(expert_count, local_count, CAP, 1).astype(jnp.float32)
    gate_pre = jnp.einsum("slcd,ldf->slcf", rows_in, w_gate, preferred_element_type=jnp.float32)
    up_pre = jnp.einsum("slcd,ldf->slcf", rows_in, w_up, preferred_element_type=jnp.float32)
    hidden_grad = jnp.einsum("slcd,lfd->slcf", grads_in, w_down, preferred_element_type=jnp.float32)
    sigma = jax.nn.sigmoid(gate_pre)
    activated = gate_pre * sigma
    hidden = activated * up_pre
    inner_part = jnp.sum(hidden * hidden_grad, axis=3)
    weighted = (row_probs * hidden).astype(jnp.bfloat16)
    scaled = row_probs * hidden_grad
    gate_grad = (scaled * up_pre * sigma * (1.0 + gate_pre * (1.0 - sigma))).astype(jnp.bfloat16)
    up_grad = (scaled * activated).astype(jnp.bfloat16)
    row_part = jnp.einsum("slcf,ldf->slcd", gate_grad, w_gate, preferred_element_type=jnp.float32)
    row_part = row_part + jnp.einsum(
        "slcf,ldf->slcd", up_grad, w_up, preferred_element_type=jnp.float32
    )
    gate_total = jnp.einsum(
        "slcd,slcf->ldf", rows_in, gate_grad, preferred_element_type=jnp.float32
    )
    up_total = jnp.einsum("slcd,slcf->ldf", rows_in, up_grad, preferred_element_type=jnp.float32)
    down_total = jnp.einsum(
        "slcf,slcd->lfd", weighted, grads_in, preferred_element_type=jnp.float32
    )
    lanes = experts * CAP
    own_part = lax.psum_scatter(
        row_part.astype(jnp.bfloat16), "tensor", scatter_dimension=3, tiled=True
    ).astype(jnp.float32)
    inner_sum = lax.psum(inner_part.astype(jnp.bfloat16), "tensor").astype(jnp.float32)
    quarter = own_part.shape[3]
    returned_rows, returned_inner = (
        lax.all_to_all(
            own_part.reshape(experts, CAP, quarter).astype(jnp.bfloat16),
            "expert",
            split_axis=0,
            concat_axis=0,
            tiled=True,
        ).astype(jnp.float32),
        lax.all_to_all(
            inner_sum.reshape(experts, CAP).astype(jnp.bfloat16),
            "expert",
            split_axis=0,
            concat_axis=0,
            tiled=True,
        ).astype(jnp.float32),
    )
    placing_wide = jnp.sum(matches.astype(jnp.int32), axis=2).astype(jnp.float32)
    token_grad = lax.dot_general(
        placing_wide,
        returned_rows.reshape(lanes, quarter),
        (((0,), (0,)), ((), ())),
        precision=lax.Precision.HIGHEST,
        preferred_element_type=jnp.float32,
    )
    grad_probs = jnp.sum(
        jnp.where(matches, returned_inner.reshape(lanes)[:, None, None], 0.0), axis=0
    )
    gate_sum, up_sum, down_sum = (
        lax.psum(gate_total.astype(jnp.bfloat16), "dp").astype(jnp.float32),
        lax.psum(up_total.astype(jnp.bfloat16), "dp").astype(jnp.float32),
        lax.psum(down_total.astype(jnp.bfloat16), "dp").astype(jnp.float32),
    )
    return (
        token_grad.astype(jnp.bfloat16),
        grad_probs,
        gate_sum.astype(jnp.bfloat16),
        up_sum.astype(jnp.bfloat16),
        down_sum.astype(jnp.bfloat16),
    )


def body(activations, out_grad, expert_ids, gate_probs, w_gate, w_up, w_down):
    n_expert, n_tensor, n_dp = (lax.axis_size(a) for a in ("expert", "tensor", "dp"))
    local_count, d, ff = w_gate.shape
    rows, top = expert_ids.shape
    tokens = rows * n_expert * n_dp
    wide = d // n_tensor
    own = local_count // n_dp
    e, t, p = (lax.axis_index(a) for a in ("expert", "tensor", "dp"))
    first = p * own
    scalars = jnp.stack([first, t, e * local_count + first, own - first]).astype(jnp.int32)
    meta = jnp.concatenate([expert_ids.astype(jnp.bfloat16), gate_probs], axis=1)
    meta = jnp.pad(meta, ((0, 0), (0, META - 2 * top)))
    packed = jnp.concatenate([activations, out_grad, meta], axis=1)
    w_in, w_out = load_weights(scalars, w_gate, w_up, w_down, own)
    along = [packed] + [shift(packed, "expert", k) for k in range(1, n_expert)]
    along[1], w_in, w_out = lax.optimization_barrier((along[1], w_in, w_out))
    shards, places = [], []
    for side in range(n_tensor):
        for k in range(n_expert):
            shards.append(along[k] if side == 0 else shift(along[k], "tensor", 1))
            places.append((k * rows, side))
    for i in range(n_expert * n_tensor):
        shards.append(shift(shards[i], "dp", 1))
        places.append((tokens // 2 + places[i][0], places[i][1]))
    x, og, grads, kept, sent = forward(
        shards, tuple(places), scalars, w_in, w_out, own, tokens, n_tensor, top
    )
    got = shift(sent, "dp", 1)
    got_grads = shift(grads, "dp", 1)
    half = (tokens // 2, wide + META)
    here, there = pl.pallas_call(
        dp_sum_kernel,
        in_specs=[VMEM] * 2,
        out_specs=[VMEM] * 2,
        out_shape=[pltpu.VMEM(half, jnp.float32), pltpu.VMEM(half, jnp.bfloat16)],
        name="sum_over_cores",
    )(kept, *near(got))
    crossed = shift(there, "tensor", 1)
    outputs = weight_grads(scalars, x, og, grads, local_count)
    crossed, outputs = lax.optimization_barrier((crossed, outputs))
    piece = (rows, wide + META)
    pieces = pl.pallas_call(
        tensor_sum_kernel,
        in_specs=[VMEM] * 2,
        out_specs=[VMEM] * n_expert,
        out_shape=[pltpu.VMEM(piece, jnp.float32)] + [pltpu.VMEM(piece, jnp.bfloat16)] * (n_expert - 1),
        name="sum_over_tensor",
    )(here, *near(crossed))
    received = [shift(pieces[k], "expert", -k) for k in range(1, n_expert)]
    outputs = weight_grads(scalars[3:], x, og, got_grads, local_count, outputs)
    received, outputs = lax.optimization_barrier((received, outputs))
    grad, probs = pl.pallas_call(
        functools.partial(finish_kernel, top),
        in_specs=[VMEM] * (n_expert + 1),
        out_specs=[VMEM] * 2,
        out_shape=[jax.ShapeDtypeStruct((rows, wide), jnp.bfloat16), jax.ShapeDtypeStruct((rows, top), jnp.float32)],
        name="sum_over_experts",
    )(expert_ids, pieces[0], *near(*received))
    return (grad, probs, *outputs)


def solution(mesh):
    in_specs = (
        P(("groups", "expert", "dp"), "tensor"),
        P(("groups", "expert", "dp"), "tensor"),
        P(("groups", "expert", "dp"), None),
        P(("groups", "expert", "dp"), None),
        P("expert", None, "tensor"),
        P("expert", None, "tensor"),
        P("expert", "tensor", None),
    )
    out_specs = (
        P(("groups", "expert", "dp"), "tensor"),
        P(("groups", "expert", "dp"), None),
        P(("groups", "expert"), None, "tensor"),
        P(("groups", "expert"), None, "tensor"),
        P(("groups", "expert"), "tensor", None),
    )
    sizes = dict(mesh.shape)
    compact = sizes["expert"] <= 4 and sizes["tensor"] == 2 and sizes["dp"] == 2
    return jax.shard_map(body if compact else general_body, mesh=mesh, in_specs=in_specs, out_specs=out_specs, check_vma=False)
```

```python
import functools

import jax
import jax.numpy as jnp
from jax import lax
from jax.experimental import pallas as pl
from jax.experimental.pallas import tpu as pltpu
from jax.sharding import PartitionSpec as P

CAP = 16
META = 128
PARTS = 2
MIB = 1024 * 1024
NT = (((1,), (1,)), ((), ()))
TN = (((0,), (0,)), ((), ()))
ANY = pl.BlockSpec(memory_space=pl.ANY)
SMEM = pl.BlockSpec(memory_space=pltpu.SMEM)
VMEM = pl.BlockSpec(memory_space=pltpu.VMEM)


def near(*arrays):
    return [pltpu.with_memory_space_constraint(x, pltpu.VMEM) for x in arrays]


def far(*arrays):
    return [pltpu.with_memory_space_constraint(x, pltpu.HBM) for x in arrays]


def pack_kernel(top, act_hbm, og_hbm, ids_hbm, probs_hbm, out_ref, ids_ref, probs_ref, sems):
    rows, wide = act_hbm.shape
    copies = [
        pltpu.make_async_copy(act_hbm, out_ref.at[:, :wide], sems.at[0]),
        pltpu.make_async_copy(og_hbm, out_ref.at[:, wide : 2 * wide], sems.at[1]),
        pltpu.make_async_copy(ids_hbm, ids_ref, sems.at[2]),
        pltpu.make_async_copy(probs_hbm, probs_ref, sems.at[3]),
    ]
    for copy in copies:
        copy.start()
    for copy in copies[2:]:
        copy.wait()
    meta = jnp.concatenate([ids_ref[...].astype(jnp.float32), probs_ref[...].astype(jnp.float32)], axis=0)
    meta = jnp.concatenate([meta, jnp.zeros((META - 2 * top, rows), jnp.float32)], axis=0)
    out_ref[:, 2 * wide :] = meta.T.astype(jnp.bfloat16)
    for copy in copies[:2]:
        copy.wait()


def pack(activations, out_grad, ids, probs):
    rows, wide = activations.shape
    return pl.pallas_call(
        functools.partial(pack_kernel, ids.shape[0]),
        in_specs=[ANY] * 4,
        out_specs=VMEM,
        out_shape=pltpu.VMEM((rows, 2 * wide + META), jnp.bfloat16),
        scratch_shapes=[
            pltpu.VMEM(ids.shape, ids.dtype),
            pltpu.VMEM(probs.shape, probs.dtype),
            pltpu.SemaphoreType.DMA((4,)),
        ],
        compiler_params=pltpu.CompilerParams(vmem_limit_bytes=4 * MIB),
        name="pack_tokens",
    )(*far(activations, out_grad, ids, probs))


def load_kernel(by_row, first_ref, *refs):
    *sources, target_ref, sem = refs
    copies = []
    count, step = len(sources), sources[0].shape[1 if by_row else 2]
    for i in range(target_ref.shape[0 if by_row else 1] // (count * step)):
        for j, source in enumerate(sources):
            at = pl.ds((count * i + j) * step, step)
            target = target_ref.at[at, :] if by_row else target_ref.at[:, at]
            copies.append(pltpu.make_async_copy(source.at[first_ref[0] + i], target, sem))
    for copy in copies:
        copy.start()
    for copy in copies:
        copy.wait()


def load_weights(first, sources, count, by_row):
    _, rows, columns = sources[0].shape
    many = count * len(sources)
    shape = (many * rows, columns) if by_row else (rows, many * columns)
    return pl.pallas_call(
        functools.partial(load_kernel, by_row),
        in_specs=[SMEM] + [ANY] * len(sources),
        out_specs=VMEM,
        out_shape=pltpu.VMEM(shape, jnp.bfloat16),
        scratch_shapes=[pltpu.SemaphoreType.DMA],
        compiler_params=pltpu.CompilerParams(vmem_limit_bytes=4 * MIB),
        cost_estimate=pl.CostEstimate(flops=0, bytes_accessed=2 * many * rows * columns, transcendentals=0),
        name="load_weights",
    )(first, *far(*sources))


def forward_kernel(places, n_tensor, top, own, scalars, *refs):
    count = len(places)
    shards, (w_in, w_out) = refs[:count], refs[count : count + 2]
    x_ref, og_ref, grads_ref, kept_ref, sent_ref, meta_ref = refs[count + 2 :]
    tensor = scalars[1]
    tokens, d = x_ref.shape
    wide, share = d // n_tensor, tokens // 2
    ff = w_out.shape[0] // own
    for shard, (row, side) in zip(shards, places):
        rows = shard.shape[0]
        columns = pl.ds(pl.multiple_of(lax.rem(tensor + side, n_tensor) * wide, wide), wide)
        x_ref[pl.ds(row, rows), columns] = shard[:, :wide]
        og_ref[pl.ds(row, rows), columns] = shard[:, wide : 2 * wide]
        if side == 0:
            meta_ref[pl.ds(row, rows), :] = shard[:, 2 * wide :].astype(jnp.float32)
    pre = jnp.dot(x_ref[...], w_in[...], preferred_element_type=jnp.float32)
    hidden_grads = lax.dot_general(og_ref[...], w_out[...], NT, preferred_element_type=jnp.float32)
    meta = meta_ref[...]
    lane = lax.broadcasted_iota(jnp.int32, meta.shape, 1)
    inners = jnp.zeros(meta.shape, jnp.float32)
    both = []
    for i in range(own):
        gate_pre, up_pre = pre[:, 2 * i * ff : (2 * i + 1) * ff], pre[:, (2 * i + 1) * ff : (2 * i + 2) * ff]
        hidden_grad = hidden_grads[:, i * ff : (i + 1) * ff]
        expert = scalars[2] + i
        hit = meta[:, :top] == expert.astype(jnp.float32)
        prob = jnp.sum(jnp.where(hit, meta[:, top : 2 * top], 0.0), axis=1, keepdims=True)
        sigma = jax.nn.sigmoid(gate_pre)
        activated = gate_pre * sigma
        hidden = activated * up_pre
        inner = jnp.sum(hidden * hidden_grad, axis=1, keepdims=True)
        inners = jnp.where(lane == expert, inner, inners)
        scaled = prob * hidden_grad
        gate_grad = (scaled * up_pre * sigma * (1.0 + gate_pre * (1.0 - sigma))).astype(jnp.bfloat16)
        up_grad = (scaled * activated).astype(jnp.bfloat16)
        grads_ref[i, :, :ff] = gate_grad
        grads_ref[i, :, ff : 2 * ff] = up_grad
        grads_ref[i, :, 2 * ff :] = (prob * hidden).astype(jnp.bfloat16)
        both += [gate_grad, up_grad]
    both = jnp.concatenate(both, axis=1)
    for side in range(n_tensor):
        at = pl.ds(pl.multiple_of(lax.rem(tensor + side, n_tensor) * wide, wide), wide)
        total = lax.dot_general(both, w_in[at, :], NT, preferred_element_type=jnp.float32)
        kept_ref[side, :, :wide] = total[:share]
        kept_ref[side, :, wide:] = inners[:share]
        sent_ref[side, :, :wide] = total[share:].astype(jnp.bfloat16)
        sent_ref[side, :, wide:] = inners[share:].astype(jnp.bfloat16)


def forward(shards, places, scalars, weights, own, tokens, n_tensor, top):
    d, ff = weights[1].shape[1], weights[1].shape[0] // own
    sums = (n_tensor, tokens // 2, d // n_tensor + META)
    return pl.pallas_call(
        functools.partial(forward_kernel, places, n_tensor, top, own),
        in_specs=[SMEM] + [VMEM] * (len(shards) + 2),
        out_specs=[VMEM] * 5,
        out_shape=[
            pltpu.VMEM((tokens, d), jnp.bfloat16),
            pltpu.VMEM((tokens, d), jnp.bfloat16),
            pltpu.VMEM((own, tokens, 3 * ff), jnp.bfloat16),
            pltpu.VMEM(sums, jnp.float32),
            pltpu.VMEM(sums, jnp.bfloat16),
        ],
        scratch_shapes=[pltpu.VMEM((tokens, META), jnp.float32)],
        compiler_params=pltpu.CompilerParams(vmem_limit_bytes=16 * MIB),
        cost_estimate=pl.CostEstimate(
            flops=10 * own * tokens * d * ff, bytes_accessed=16 * tokens * d, transcendentals=0
        ),
        name="routed_forward",
    )(scalars, *near(*shards, *weights))


def weight_kernel(swap, first_ref, x_ref, og_ref, grads_ref, *refs):
    *targets, gate_ref, up_ref, down_ref, sem = refs[-7:]
    own, d, ff = gate_ref.shape
    half, step = grads_ref.shape[1] // 2, d // PARTS
    copies = []

    def send(ref, target, i, at):
        copies.append(pltpu.make_async_copy(ref.at[(i, *at)], target.at[(first_ref[0] + i, *at)], sem))
        copies[-1].start()

    for i in range(own):
        grads = grads_ref[i]
        if swap:
            grads = jnp.concatenate([grads[half:], grads[:half]], axis=0)
        for part in range(PARTS):
            at, every = pl.ds(part * step, step), pl.ds(0, ff)
            total = lax.dot_general(x_ref[:, at], grads[:, : 2 * ff], TN, preferred_element_type=jnp.float32)
            gate_ref[i, at, :] = total[:, :ff].astype(jnp.bfloat16)
            up_ref[i, at, :] = total[:, ff:].astype(jnp.bfloat16)
            send(gate_ref, targets[0], i, (at, every))
            send(up_ref, targets[1], i, (at, every))
        for part in range(PARTS):
            at, every = pl.ds(part * step, step), pl.ds(0, ff)
            total = lax.dot_general(grads[:, 2 * ff :], og_ref[:, at], TN, preferred_element_type=jnp.float32)
            down_ref[i, :, at] = total.astype(jnp.bfloat16)
            send(down_ref, targets[2], i, (every, at))
    for copy in copies:
        copy.wait()


def weight_grads(first, x, og, grads, local_count, into=None):
    own, tokens, ff = grads.shape[0], grads.shape[1], grads.shape[2] // 3
    d = x.shape[1]
    kept = [] if into is None else list(into)
    shapes = [(d, ff), (d, ff), (ff, d)]
    return pl.pallas_call(
        functools.partial(weight_kernel, into is not None),
        in_specs=[SMEM] + [VMEM] * 3 + [ANY] * len(kept),
        out_specs=[ANY] * 3,
        out_shape=[pltpu.HBM((local_count, *s), jnp.bfloat16) for s in shapes],
        scratch_shapes=[pltpu.VMEM((own, *s), jnp.bfloat16) for s in shapes] + [pltpu.SemaphoreType.DMA],
        input_output_aliases={4 + i: i for i in range(len(kept))},
        compiler_params=pltpu.CompilerParams(vmem_limit_bytes=26 * MIB),
        cost_estimate=pl.CostEstimate(
            flops=6 * own * tokens * d * ff, bytes_accessed=6 * own * d * ff, transcendentals=0
        ),
        name="weight_grads",
    )(first, *near(x, og, grads), *kept)


def dp_sum_kernel(kept_ref, got_ref, here_ref, there_ref):
    here_ref[...] = kept_ref[0] + got_ref[0].astype(jnp.float32)
    there_ref[...] = (kept_ref[1] + got_ref[1].astype(jnp.float32)).astype(jnp.bfloat16)


def tensor_sum_kernel(here_ref, got_ref, own_ref, *out_refs):
    rows = own_ref.shape[0]
    for block, target in enumerate((own_ref, *out_refs)):
        at = pl.ds(block * rows, rows)
        target[...] = (here_ref[at, :] + got_ref[at, :].astype(jnp.float32)).astype(target.dtype)


def finish_kernel(top, ids_ref, own_ref, *refs):
    parts, (grad_ref, probs_ref) = refs[:-2], refs[-2:]
    total = own_ref[...]
    for part in parts:
        total = total + part[...].astype(jnp.float32)
    wide = grad_ref.shape[1]
    grad_ref[...] = total[:, :wide].astype(jnp.bfloat16)
    inner = total[:, wide:].T
    ids = ids_ref[...]
    expert = lax.broadcasted_iota(jnp.int32, inner.shape, 0)
    for k in range(top):
        picked = jnp.where(expert == ids[k : k + 1, :], inner, 0.0)
        probs_ref[k : k + 1, :] = jnp.sum(picked, axis=0, keepdims=True)


def shift(x, axis, by):
    count = lax.axis_size(axis)
    return lax.ppermute(x, axis, [(i, (i + by) % count) for i in range(count)])


def general_body(activations, out_grad, expert_ids, gate_probs, w_gate, w_up, w_down):
    d = activations.shape[1] * lax.axis_size("tensor")
    expert_count = lax.axis_size("expert")
    local_count = w_gate.shape[0]
    experts = expert_count * local_count
    token_rows = expert_ids.shape[0]
    flat_ids = expert_ids.reshape(-1)
    onehot = (flat_ids[:, None] == jnp.arange(experts, dtype=jnp.int32)[None, :]).astype(jnp.int32)
    before = jnp.cumsum(onehot, axis=0) - onehot
    slot_index = jnp.sum(before * onehot, axis=1)
    position = (flat_ids * CAP + slot_index).reshape(token_rows, expert_ids.shape[1])
    lane_index = jnp.arange(experts * CAP, dtype=jnp.int32)
    matches = position[None, :, :] == lane_index[:, None, None]
    placing = jnp.sum(matches.astype(jnp.int32), axis=2).astype(jnp.bfloat16)
    send_probs = jnp.sum(jnp.where(matches, gate_probs.astype(jnp.float32)[None], 0.0), axis=(1, 2))
    send_probs = send_probs.astype(jnp.bfloat16).reshape(experts, CAP)
    full_rows, full_grads = (
        lax.all_gather(activations, "tensor", axis=1, tiled=True),
        lax.all_gather(out_grad, "tensor", axis=1, tiled=True),
    )
    send_rows = (
        jnp.dot(placing, full_rows, preferred_element_type=jnp.float32)
        .astype(jnp.bfloat16)
        .reshape(experts, CAP, d)
    )
    send_grads = (
        jnp.dot(placing, full_grads, preferred_element_type=jnp.float32)
        .astype(jnp.bfloat16)
        .reshape(experts, CAP, d)
    )
    got_rows, got_grads, got_probs = (
        lax.all_to_all(send_rows, "expert", split_axis=0, concat_axis=0, tiled=True),
        lax.all_to_all(send_grads, "expert", split_axis=0, concat_axis=0, tiled=True),
        lax.all_to_all(send_probs, "expert", split_axis=0, concat_axis=0, tiled=True),
    )
    rows_in = got_rows.reshape(expert_count, local_count, CAP, d)
    grads_in = got_grads.reshape(expert_count, local_count, CAP, d)
    row_probs = got_probs.reshape(expert_count, local_count, CAP, 1).astype(jnp.float32)
    gate_pre = jnp.einsum("slcd,ldf->slcf", rows_in, w_gate, preferred_element_type=jnp.float32)
    up_pre = jnp.einsum("slcd,ldf->slcf", rows_in, w_up, preferred_element_type=jnp.float32)
    hidden_grad = jnp.einsum("slcd,lfd->slcf", grads_in, w_down, preferred_element_type=jnp.float32)
    sigma = jax.nn.sigmoid(gate_pre)
    activated = gate_pre * sigma
    hidden = activated * up_pre
    inner_part = jnp.sum(hidden * hidden_grad, axis=3)
    weighted = (row_probs * hidden).astype(jnp.bfloat16)
    scaled = row_probs * hidden_grad
    gate_grad = (scaled * up_pre * sigma * (1.0 + gate_pre * (1.0 - sigma))).astype(jnp.bfloat16)
    up_grad = (scaled * activated).astype(jnp.bfloat16)
    row_part = jnp.einsum("slcf,ldf->slcd", gate_grad, w_gate, preferred_element_type=jnp.float32)
    row_part = row_part + jnp.einsum(
        "slcf,ldf->slcd", up_grad, w_up, preferred_element_type=jnp.float32
    )
    gate_total = jnp.einsum(
        "slcd,slcf->ldf", rows_in, gate_grad, preferred_element_type=jnp.float32
    )
    up_total = jnp.einsum("slcd,slcf->ldf", rows_in, up_grad, preferred_element_type=jnp.float32)
    down_total = jnp.einsum(
        "slcf,slcd->lfd", weighted, grads_in, preferred_element_type=jnp.float32
    )
    lanes = experts * CAP
    own_part = lax.psum_scatter(
        row_part.astype(jnp.bfloat16), "tensor", scatter_dimension=3, tiled=True
    ).astype(jnp.float32)
    inner_sum = lax.psum(inner_part.astype(jnp.bfloat16), "tensor").astype(jnp.float32)
    quarter = own_part.shape[3]
    returned_rows, returned_inner = (
        lax.all_to_all(
            own_part.reshape(experts, CAP, quarter).astype(jnp.bfloat16),
            "expert",
            split_axis=0,
            concat_axis=0,
            tiled=True,
        ).astype(jnp.float32),
        lax.all_to_all(
            inner_sum.reshape(experts, CAP).astype(jnp.bfloat16),
            "expert",
            split_axis=0,
            concat_axis=0,
            tiled=True,
        ).astype(jnp.float32),
    )
    placing_wide = jnp.sum(matches.astype(jnp.int32), axis=2).astype(jnp.float32)
    token_grad = lax.dot_general(
        placing_wide,
        returned_rows.reshape(lanes, quarter),
        (((0,), (0,)), ((), ())),
        precision=lax.Precision.HIGHEST,
        preferred_element_type=jnp.float32,
    )
    grad_probs = jnp.sum(
        jnp.where(matches, returned_inner.reshape(lanes)[:, None, None], 0.0), axis=0
    )
    gate_sum, up_sum, down_sum = (
        lax.psum(gate_total.astype(jnp.bfloat16), "dp").astype(jnp.float32),
        lax.psum(up_total.astype(jnp.bfloat16), "dp").astype(jnp.float32),
        lax.psum(down_total.astype(jnp.bfloat16), "dp").astype(jnp.float32),
    )
    return (
        token_grad.astype(jnp.bfloat16),
        grad_probs,
        gate_sum.astype(jnp.bfloat16),
        up_sum.astype(jnp.bfloat16),
        down_sum.astype(jnp.bfloat16),
    )


def body(activations, out_grad, expert_ids, gate_probs, w_gate, w_up, w_down):
    n_expert, n_tensor, n_dp = (lax.axis_size(a) for a in ("expert", "tensor", "dp"))
    local_count, d, ff = w_gate.shape
    rows, top = expert_ids.shape
    tokens = rows * n_expert * n_dp
    wide = d // n_tensor
    own = local_count // n_dp
    e, t, p = (lax.axis_index(a) for a in ("expert", "tensor", "dp"))
    first = p * own
    scalars = jnp.stack([first, t, e * local_count + first, own - first]).astype(jnp.int32)
    ids = expert_ids.T
    packed = pack(activations, out_grad, ids, gate_probs.T)
    along = [packed] + [shift(packed, "expert", k) for k in range(1, n_expert)]
    w_in = load_weights(scalars, (w_gate, w_up), own, False)
    along[3], w_in, then = lax.optimization_barrier((along[3], w_in, scalars))
    across = [shift(along[0], "tensor", 1), None, None, shift(along[3], "tensor", 1)]
    w_out = load_weights(then, (w_down,), own, True)
    along[1], along[2], w_out = lax.optimization_barrier((along[1], along[2], w_out))
    across[1], across[2] = (shift(x, "tensor", 1) for x in along[1:3])
    shards = along + across
    places = [(k * rows, side) for side in range(n_tensor) for k in range(n_expert)]
    for i in range(n_expert * n_tensor):
        shards.append(shift(shards[i], "dp", 1))
        places.append((tokens // 2 + places[i][0], places[i][1]))
    x, og, grads, kept, sent = forward(
        shards, tuple(places), scalars, (w_in, w_out), own, tokens, n_tensor, top
    )
    got = shift(sent, "dp", 1)
    got, grads = lax.optimization_barrier((got, grads))
    got_grads = shift(grads, "dp", 1)
    half = (tokens // 2, wide + META)
    here, there = pl.pallas_call(
        dp_sum_kernel,
        in_specs=[VMEM] * 2,
        out_specs=[VMEM] * 2,
        out_shape=[pltpu.VMEM(half, jnp.float32), pltpu.VMEM(half, jnp.bfloat16)],
        compiler_params=pltpu.CompilerParams(vmem_limit_bytes=4 * MIB),
        name="sum_over_cores",
    )(kept, *near(got))
    crossed = shift(there, "tensor", 1)
    outputs = weight_grads(scalars, x, og, grads, local_count)
    crossed, outputs = lax.optimization_barrier((crossed, outputs))
    piece = (rows, wide + META)
    pieces = pl.pallas_call(
        tensor_sum_kernel,
        in_specs=[VMEM] * 2,
        out_specs=[VMEM] * n_expert,
        out_shape=[pltpu.VMEM(piece, jnp.float32)] + [pltpu.VMEM(piece, jnp.bfloat16)] * (n_expert - 1),
        compiler_params=pltpu.CompilerParams(vmem_limit_bytes=4 * MIB),
        name="sum_over_tensor",
    )(here, *near(crossed))
    received = [shift(pieces[k], "expert", -k) for k in range(1, n_expert)]
    outputs = weight_grads(scalars[3:], x, og, got_grads, local_count, outputs)
    received, outputs = lax.optimization_barrier((received, outputs))
    grad, probs = pl.pallas_call(
        functools.partial(finish_kernel, top),
        in_specs=[VMEM] * (n_expert + 1),
        out_specs=[VMEM] * 2,
        out_shape=[jax.ShapeDtypeStruct((rows, wide), jnp.bfloat16), jax.ShapeDtypeStruct((top, rows), jnp.float32)],
        compiler_params=pltpu.CompilerParams(vmem_limit_bytes=4 * MIB),
        name="sum_over_experts",
    )(ids, pieces[0], *near(*received))
    return (grad, probs.T, *outputs)


def solution(mesh):
    in_specs = (
        P(("groups", "expert", "dp"), "tensor"),
        P(("groups", "expert", "dp"), "tensor"),
        P(("groups", "expert", "dp"), None),
        P(("groups", "expert", "dp"), None),
        P("expert", None, "tensor"),
        P("expert", None, "tensor"),
        P("expert", "tensor", None),
    )
    out_specs = (
        P(("groups", "expert", "dp"), "tensor"),
        P(("groups", "expert", "dp"), None),
        P(("groups", "expert"), None, "tensor"),
        P(("groups", "expert"), None, "tensor"),
        P(("groups", "expert"), "tensor", None),
    )
    sizes = dict(mesh.shape)
    compact = sizes["expert"] == 4 and sizes["tensor"] == 2 and sizes["dp"] == 2
    return jax.shard_map(body if compact else general_body, mesh=mesh, in_specs=in_specs, out_specs=out_specs, check_vma=False)
```

```python
import functools

import jax
import jax.numpy as jnp
from jax import lax
from jax.experimental import pallas as pl
from jax.experimental.pallas import tpu as pltpu
from jax.sharding import PartitionSpec as P

CAP = 16
META = 128
PARTS = 2
MIB = 1024 * 1024
NT = (((1,), (1,)), ((), ()))
TN = (((0,), (0,)), ((), ()))
ANY = pl.BlockSpec(memory_space=pl.ANY)
SMEM = pl.BlockSpec(memory_space=pltpu.SMEM)
VMEM = pl.BlockSpec(memory_space=pltpu.VMEM)
LIGHT = pl.CostEstimate(flops=0, bytes_accessed=1024, transcendentals=0)


def near(*arrays):
    return [pltpu.with_memory_space_constraint(x, pltpu.VMEM) for x in arrays]


def far(*arrays):
    return [pltpu.with_memory_space_constraint(x, pltpu.HBM) for x in arrays]


def pack_kernel(top, act_hbm, og_hbm, ids_hbm, probs_hbm, out_ref, ids_ref, probs_ref, sems):
    rows, wide = act_hbm.shape
    copies = [
        pltpu.make_async_copy(act_hbm, out_ref.at[:, :wide], sems.at[0]),
        pltpu.make_async_copy(og_hbm, out_ref.at[:, wide : 2 * wide], sems.at[1]),
        pltpu.make_async_copy(ids_hbm, ids_ref, sems.at[2]),
        pltpu.make_async_copy(probs_hbm, probs_ref, sems.at[3]),
    ]
    for copy in copies:
        copy.start()
    for copy in copies[2:]:
        copy.wait()
    meta = jnp.concatenate([ids_ref[...].astype(jnp.float32), probs_ref[...].astype(jnp.float32)], axis=0)
    meta = jnp.concatenate([meta, jnp.zeros((META - 2 * top, rows), jnp.float32)], axis=0)
    out_ref[:, 2 * wide :] = meta.T.astype(jnp.bfloat16)
    for copy in copies[:2]:
        copy.wait()


def pack(activations, out_grad, ids, probs):
    rows, wide = activations.shape
    return pl.pallas_call(
        functools.partial(pack_kernel, ids.shape[0]),
        in_specs=[ANY] * 4,
        out_specs=VMEM,
        out_shape=pltpu.VMEM((rows, 2 * wide + META), jnp.bfloat16),
        scratch_shapes=[
            pltpu.VMEM(ids.shape, ids.dtype),
            pltpu.VMEM(probs.shape, probs.dtype),
            pltpu.SemaphoreType.DMA((4,)),
        ],
        compiler_params=pltpu.CompilerParams(vmem_limit_bytes=4 * MIB),
        name="pack_tokens",
    )(*far(activations, out_grad, ids, probs))


def collect_kernel(*refs):
    *shards, out_ref = refs
    rows = shards[0].shape[0]
    for i, shard in enumerate(shards):
        out_ref[pl.ds(i * rows, rows), :] = shard[...]


def collect(shards):
    rows, columns = shards[0].shape
    return pl.pallas_call(
        collect_kernel,
        in_specs=[VMEM] * len(shards),
        out_specs=VMEM,
        out_shape=pltpu.VMEM((len(shards) * rows, columns), shards[0].dtype),
        compiler_params=pltpu.CompilerParams(vmem_limit_bytes=4 * MIB),
        cost_estimate=LIGHT,
        name="collect",
    )(*near(*shards))


def load_kernel(count, start, first_ref, wg_ref, wu_ref, *refs):
    target_ref, sem = refs[-2:]
    ff = wg_ref.shape[2]
    copies = []
    for i in range(start, start + count):
        for j, source in enumerate((wg_ref, wu_ref)):
            target = target_ref.at[:, pl.ds((2 * i + j) * ff, ff)]
            copies.append(pltpu.make_async_copy(source.at[first_ref[0] + i], target, sem))
    for copy in copies:
        copy.start()
    for copy in copies:
        copy.wait()


def load_weights(first, w_gate, w_up, own, count, into=None):
    _, d, ff = w_gate.shape
    kept = [] if into is None else near(into)
    return pl.pallas_call(
        functools.partial(load_kernel, own - count if kept else count, count if kept else 0),
        in_specs=[SMEM, ANY, ANY] + [VMEM] * len(kept),
        out_specs=VMEM,
        out_shape=pltpu.VMEM((d, own * 2 * ff), jnp.bfloat16),
        scratch_shapes=[pltpu.SemaphoreType.DMA],
        input_output_aliases={3: 0} if kept else {},
        compiler_params=pltpu.CompilerParams(vmem_limit_bytes=4 * MIB),
        cost_estimate=LIGHT,
        name="load_weights",
    )(first, *far(w_gate, w_up), *kept)


def forward_kernel(places, n_tensor, top, own, scalars, *refs):
    count = len(places)
    shards, (w_in, wd_ref) = refs[:count], refs[count : count + 2]
    x_ref, og_ref, grads_ref, kept_ref, sent_ref, meta_ref, w_out, sem = refs[count + 2 :]
    tensor = scalars[1]
    tokens, d = x_ref.shape
    wide, share = d // n_tensor, tokens // 2
    ff = wd_ref.shape[1]
    copies = [
        pltpu.make_async_copy(wd_ref.at[scalars[0] + i], w_out.at[pl.ds(i * ff, ff), :], sem) for i in range(own)
    ]
    for copy in copies:
        copy.start()
    for shard, held in zip(shards, places):
        rows = shard.shape[0] // len(held)
        for i, (row, side) in enumerate(held):
            at = pl.ds(i * rows, rows)
            columns = pl.ds(pl.multiple_of(lax.rem(tensor + side, n_tensor) * wide, wide), wide)
            x_ref[pl.ds(row, rows), columns] = shard[at, :wide]
            og_ref[pl.ds(row, rows), columns] = shard[at, wide : 2 * wide]
            if side == 0:
                meta_ref[pl.ds(row, rows), :] = shard[at, 2 * wide :].astype(jnp.float32)
    pre = jnp.dot(x_ref[...], w_in[...], preferred_element_type=jnp.float32)
    for copy in copies:
        copy.wait()
    hidden_grads = lax.dot_general(og_ref[...], w_out[...], NT, preferred_element_type=jnp.float32)
    meta = meta_ref[...]
    lane = lax.broadcasted_iota(jnp.int32, meta.shape, 1)
    inners = jnp.zeros(meta.shape, jnp.float32)
    both = []
    for i in range(own):
        gate_pre, up_pre = pre[:, 2 * i * ff : (2 * i + 1) * ff], pre[:, (2 * i + 1) * ff : (2 * i + 2) * ff]
        hidden_grad = hidden_grads[:, i * ff : (i + 1) * ff]
        expert = scalars[2] + i
        hit = meta[:, :top] == expert.astype(jnp.float32)
        prob = jnp.sum(jnp.where(hit, meta[:, top : 2 * top], 0.0), axis=1, keepdims=True)
        sigma = jax.nn.sigmoid(gate_pre)
        activated = gate_pre * sigma
        hidden = activated * up_pre
        inner = jnp.sum(hidden * hidden_grad, axis=1, keepdims=True)
        inners = jnp.where(lane == expert, inner, inners)
        scaled = prob * hidden_grad
        gate_grad = (scaled * up_pre * sigma * (1.0 + gate_pre * (1.0 - sigma))).astype(jnp.bfloat16)
        up_grad = (scaled * activated).astype(jnp.bfloat16)
        grads_ref[i, :, :ff] = gate_grad
        grads_ref[i, :, ff : 2 * ff] = up_grad
        grads_ref[i, :, 2 * ff :] = (prob * hidden).astype(jnp.bfloat16)
        both += [gate_grad, up_grad]
    both = jnp.concatenate(both, axis=1)
    for side in range(n_tensor):
        at = pl.ds(pl.multiple_of(lax.rem(tensor + side, n_tensor) * wide, wide), wide)
        total = lax.dot_general(both, w_in[at, :], NT, preferred_element_type=jnp.float32)
        kept_ref[side, :, :wide] = total[:share]
        kept_ref[side, :, wide:] = inners[:share]
        sent_ref[side, :, :wide] = total[share:].astype(jnp.bfloat16)
        sent_ref[side, :, wide:] = inners[share:].astype(jnp.bfloat16)


def forward(shards, places, scalars, w_in, w_down, own, tokens, n_tensor, top):
    _, ff, d = w_down.shape
    sums = (n_tensor, tokens // 2, d // n_tensor + META)
    return pl.pallas_call(
        functools.partial(forward_kernel, places, n_tensor, top, own),
        in_specs=[SMEM] + [VMEM] * (len(shards) + 1) + [ANY],
        out_specs=[VMEM] * 5,
        out_shape=[
            pltpu.VMEM((tokens, d), jnp.bfloat16),
            pltpu.VMEM((tokens, d), jnp.bfloat16),
            pltpu.VMEM((own, tokens, 3 * ff), jnp.bfloat16),
            pltpu.VMEM(sums, jnp.float32),
            pltpu.VMEM(sums, jnp.bfloat16),
        ],
        scratch_shapes=[
            pltpu.VMEM((tokens, META), jnp.float32),
            pltpu.VMEM((own * ff, d), jnp.bfloat16),
            pltpu.SemaphoreType.DMA,
        ],
        compiler_params=pltpu.CompilerParams(vmem_limit_bytes=22 * MIB),
        cost_estimate=pl.CostEstimate(
            flops=10 * own * tokens * d * ff, bytes_accessed=16 * tokens * d, transcendentals=0
        ),
        name="routed_forward",
    )(scalars, *near(*shards, w_in), *far(w_down))


def weight_kernel(swap, first_ref, x_ref, og_ref, grads_ref, *refs):
    *targets, gate_ref, up_ref, down_ref, sem = refs[-7:]
    own, d, ff = gate_ref.shape
    half, step = grads_ref.shape[1] // 2, d // PARTS
    copies = []

    def send(ref, target, i, at):
        copies.append(pltpu.make_async_copy(ref.at[(i, *at)], target.at[(first_ref[0] + i, *at)], sem))
        copies[-1].start()

    for i in range(own):
        grads = grads_ref[i]
        if swap:
            grads = jnp.concatenate([grads[half:], grads[:half]], axis=0)
        for part in range(PARTS):
            at, every = pl.ds(part * step, step), pl.ds(0, ff)
            total = lax.dot_general(x_ref[:, at], grads[:, : 2 * ff], TN, preferred_element_type=jnp.float32)
            gate_ref[i, at, :] = total[:, :ff].astype(jnp.bfloat16)
            up_ref[i, at, :] = total[:, ff:].astype(jnp.bfloat16)
            send(gate_ref, targets[0], i, (at, every))
            send(up_ref, targets[1], i, (at, every))
        for part in range(PARTS):
            at, every = pl.ds(part * step, step), pl.ds(0, ff)
            total = lax.dot_general(grads[:, 2 * ff :], og_ref[:, at], TN, preferred_element_type=jnp.float32)
            down_ref[i, :, at] = total.astype(jnp.bfloat16)
            send(down_ref, targets[2], i, (every, at))
    for copy in copies:
        copy.wait()


def weight_grads(first, x, og, grads, local_count, into=None):
    own, tokens, ff = grads.shape[0], grads.shape[1], grads.shape[2] // 3
    d = x.shape[1]
    kept = [] if into is None else list(into)
    shapes = [(d, ff), (d, ff), (ff, d)]
    return pl.pallas_call(
        functools.partial(weight_kernel, into is not None),
        in_specs=[SMEM] + [VMEM] * 3 + [ANY] * len(kept),
        out_specs=[ANY] * 3,
        out_shape=[pltpu.HBM((local_count, *s), jnp.bfloat16) for s in shapes],
        scratch_shapes=[pltpu.VMEM((own, *s), jnp.bfloat16) for s in shapes] + [pltpu.SemaphoreType.DMA],
        input_output_aliases={4 + i: i for i in range(len(kept))},
        compiler_params=pltpu.CompilerParams(vmem_limit_bytes=26 * MIB),
        cost_estimate=pl.CostEstimate(
            flops=6 * own * tokens * d * ff, bytes_accessed=6 * own * d * ff, transcendentals=0
        ),
        name="weight_grads",
    )(first, *near(x, og, grads), *kept)


def dp_sum_kernel(kept_ref, got_ref, here_ref, there_ref):
    here_ref[...] = kept_ref[0] + got_ref[0].astype(jnp.float32)
    there_ref[...] = (kept_ref[1] + got_ref[1].astype(jnp.float32)).astype(jnp.bfloat16)


def tensor_sum_kernel(here_ref, got_ref, own_ref, *out_refs):
    rows = own_ref.shape[0]
    for block, target in enumerate((own_ref, *out_refs)):
        at = pl.ds(block * rows, rows)
        target[...] = (here_ref[at, :] + got_ref[at, :].astype(jnp.float32)).astype(target.dtype)


def finish_kernel(top, ids_ref, own_ref, *refs):
    parts, (grad_ref, probs_ref) = refs[:-2], refs[-2:]
    total = own_ref[...]
    for part in parts:
        total = total + part[...].astype(jnp.float32)
    wide = grad_ref.shape[1]
    grad_ref[...] = total[:, :wide].astype(jnp.bfloat16)
    inner = total[:, wide:].T
    ids = ids_ref[...]
    expert = lax.broadcasted_iota(jnp.int32, inner.shape, 0)
    for k in range(top):
        picked = jnp.where(expert == ids[k : k + 1, :], inner, 0.0)
        probs_ref[k : k + 1, :] = jnp.sum(picked, axis=0, keepdims=True)


def shift(x, axis, by):
    count = lax.axis_size(axis)
    return lax.ppermute(x, axis, [(i, (i + by) % count) for i in range(count)])


def general_body(activations, out_grad, expert_ids, gate_probs, w_gate, w_up, w_down):
    d = activations.shape[1] * lax.axis_size("tensor")
    expert_count = lax.axis_size("expert")
    local_count = w_gate.shape[0]
    experts = expert_count * local_count
    token_rows = expert_ids.shape[0]
    flat_ids = expert_ids.reshape(-1)
    onehot = (flat_ids[:, None] == jnp.arange(experts, dtype=jnp.int32)[None, :]).astype(jnp.int32)
    before = jnp.cumsum(onehot, axis=0) - onehot
    slot_index = jnp.sum(before * onehot, axis=1)
    position = (flat_ids * CAP + slot_index).reshape(token_rows, expert_ids.shape[1])
    lane_index = jnp.arange(experts * CAP, dtype=jnp.int32)
    matches = position[None, :, :] == lane_index[:, None, None]
    placing = jnp.sum(matches.astype(jnp.int32), axis=2).astype(jnp.bfloat16)
    send_probs = jnp.sum(jnp.where(matches, gate_probs.astype(jnp.float32)[None], 0.0), axis=(1, 2))
    send_probs = send_probs.astype(jnp.bfloat16).reshape(experts, CAP)
    full_rows, full_grads = (
        lax.all_gather(activations, "tensor", axis=1, tiled=True),
        lax.all_gather(out_grad, "tensor", axis=1, tiled=True),
    )
    send_rows = (
        jnp.dot(placing, full_rows, preferred_element_type=jnp.float32)
        .astype(jnp.bfloat16)
        .reshape(experts, CAP, d)
    )
    send_grads = (
        jnp.dot(placing, full_grads, preferred_element_type=jnp.float32)
        .astype(jnp.bfloat16)
        .reshape(experts, CAP, d)
    )
    got_rows, got_grads, got_probs = (
        lax.all_to_all(send_rows, "expert", split_axis=0, concat_axis=0, tiled=True),
        lax.all_to_all(send_grads, "expert", split_axis=0, concat_axis=0, tiled=True),
        lax.all_to_all(send_probs, "expert", split_axis=0, concat_axis=0, tiled=True),
    )
    rows_in = got_rows.reshape(expert_count, local_count, CAP, d)
    grads_in = got_grads.reshape(expert_count, local_count, CAP, d)
    row_probs = got_probs.reshape(expert_count, local_count, CAP, 1).astype(jnp.float32)
    gate_pre = jnp.einsum("slcd,ldf->slcf", rows_in, w_gate, preferred_element_type=jnp.float32)
    up_pre = jnp.einsum("slcd,ldf->slcf", rows_in, w_up, preferred_element_type=jnp.float32)
    hidden_grad = jnp.einsum("slcd,lfd->slcf", grads_in, w_down, preferred_element_type=jnp.float32)
    sigma = jax.nn.sigmoid(gate_pre)
    activated = gate_pre * sigma
    hidden = activated * up_pre
    inner_part = jnp.sum(hidden * hidden_grad, axis=3)
    weighted = (row_probs * hidden).astype(jnp.bfloat16)
    scaled = row_probs * hidden_grad
    gate_grad = (scaled * up_pre * sigma * (1.0 + gate_pre * (1.0 - sigma))).astype(jnp.bfloat16)
    up_grad = (scaled * activated).astype(jnp.bfloat16)
    row_part = jnp.einsum("slcf,ldf->slcd", gate_grad, w_gate, preferred_element_type=jnp.float32)
    row_part = row_part + jnp.einsum(
        "slcf,ldf->slcd", up_grad, w_up, preferred_element_type=jnp.float32
    )
    gate_total = jnp.einsum(
        "slcd,slcf->ldf", rows_in, gate_grad, preferred_element_type=jnp.float32
    )
    up_total = jnp.einsum("slcd,slcf->ldf", rows_in, up_grad, preferred_element_type=jnp.float32)
    down_total = jnp.einsum(
        "slcf,slcd->lfd", weighted, grads_in, preferred_element_type=jnp.float32
    )
    lanes = experts * CAP
    own_part = lax.psum_scatter(
        row_part.astype(jnp.bfloat16), "tensor", scatter_dimension=3, tiled=True
    ).astype(jnp.float32)
    inner_sum = lax.psum(inner_part.astype(jnp.bfloat16), "tensor").astype(jnp.float32)
    quarter = own_part.shape[3]
    returned_rows, returned_inner = (
        lax.all_to_all(
            own_part.reshape(experts, CAP, quarter).astype(jnp.bfloat16),
            "expert",
            split_axis=0,
            concat_axis=0,
            tiled=True,
        ).astype(jnp.float32),
        lax.all_to_all(
            inner_sum.reshape(experts, CAP).astype(jnp.bfloat16),
            "expert",
            split_axis=0,
            concat_axis=0,
            tiled=True,
        ).astype(jnp.float32),
    )
    placing_wide = jnp.sum(matches.astype(jnp.int32), axis=2).astype(jnp.float32)
    token_grad = lax.dot_general(
        placing_wide,
        returned_rows.reshape(lanes, quarter),
        (((0,), (0,)), ((), ())),
        precision=lax.Precision.HIGHEST,
        preferred_element_type=jnp.float32,
    )
    grad_probs = jnp.sum(
        jnp.where(matches, returned_inner.reshape(lanes)[:, None, None], 0.0), axis=0
    )
    gate_sum, up_sum, down_sum = (
        lax.psum(gate_total.astype(jnp.bfloat16), "dp").astype(jnp.float32),
        lax.psum(up_total.astype(jnp.bfloat16), "dp").astype(jnp.float32),
        lax.psum(down_total.astype(jnp.bfloat16), "dp").astype(jnp.float32),
    )
    return (
        token_grad.astype(jnp.bfloat16),
        grad_probs,
        gate_sum.astype(jnp.bfloat16),
        up_sum.astype(jnp.bfloat16),
        down_sum.astype(jnp.bfloat16),
    )


def body(activations, out_grad, expert_ids, gate_probs, w_gate, w_up, w_down):
    n_expert, n_tensor, n_dp = (lax.axis_size(a) for a in ("expert", "tensor", "dp"))
    local_count, d, ff = w_gate.shape
    rows, top = expert_ids.shape
    tokens = rows * n_expert * n_dp
    wide = d // n_tensor
    own = local_count // n_dp
    e, t, p = (lax.axis_index(a) for a in ("expert", "tensor", "dp"))
    first = p * own
    scalars = jnp.stack([first, t, e * local_count + first, own - first]).astype(jnp.int32)
    ids = expert_ids.T
    packed = pack(activations, out_grad, ids, gate_probs.T)
    along = [packed] + [shift(packed, "expert", k) for k in range(1, n_expert)]
    across = {k: shift(along[k], "tensor", 1) for k in (0, 3, 1)}
    along[2], across, then = lax.optimization_barrier((along[2], across, scalars))
    across[2] = shift(along[2], "tensor", 1)
    w_in = load_weights(then, w_gate, w_up, own, own // 2)
    across[2], w_in, then = lax.optimization_barrier((across[2], w_in, scalars))
    w_in = load_weights(then, w_gate, w_up, own, own // 2, w_in)
    held = collect(along + [across[k] for k in range(n_expert)])
    places = [(k * rows, side) for side in range(n_tensor) for k in range(n_expert)]
    places = [places, [(tokens // 2 + row, side) for row, side in places]]
    shards = [held, shift(held, "dp", 1)]
    x, og, grads, kept, sent = forward(
        shards, places, scalars, w_in, w_down, own, tokens, n_tensor, top
    )
    got = shift(sent, "dp", 1)
    got, grads = lax.optimization_barrier((got, grads))
    got_grads = shift(grads, "dp", 1)
    half = (tokens // 2, wide + META)
    here, there = pl.pallas_call(
        dp_sum_kernel,
        in_specs=[VMEM] * 2,
        out_specs=[VMEM] * 2,
        out_shape=[pltpu.VMEM(half, jnp.float32), pltpu.VMEM(half, jnp.bfloat16)],
        compiler_params=pltpu.CompilerParams(vmem_limit_bytes=4 * MIB),
        name="sum_over_cores",
    )(kept, *near(got))
    crossed = shift(there, "tensor", 1)
    outputs = weight_grads(scalars, x, og, grads, local_count)
    crossed, outputs = lax.optimization_barrier((crossed, outputs))
    piece = (rows, wide + META)
    pieces = pl.pallas_call(
        tensor_sum_kernel,
        in_specs=[VMEM] * 2,
        out_specs=[VMEM] * n_expert,
        out_shape=[pltpu.VMEM(piece, jnp.float32)] + [pltpu.VMEM(piece, jnp.bfloat16)] * (n_expert - 1),
        compiler_params=pltpu.CompilerParams(vmem_limit_bytes=4 * MIB),
        name="sum_over_tensor",
    )(here, *near(crossed))
    received = [shift(pieces[k], "expert", -k) for k in range(1, n_expert)]
    outputs = weight_grads(scalars[3:], x, og, got_grads, local_count, outputs)
    received, outputs = lax.optimization_barrier((received, outputs))
    grad, probs = pl.pallas_call(
        functools.partial(finish_kernel, top),
        in_specs=[VMEM] * (n_expert + 1),
        out_specs=[VMEM] * 2,
        out_shape=[jax.ShapeDtypeStruct((rows, wide), jnp.bfloat16), jax.ShapeDtypeStruct((top, rows), jnp.float32)],
        compiler_params=pltpu.CompilerParams(vmem_limit_bytes=4 * MIB),
        name="sum_over_experts",
    )(ids, pieces[0], *near(*received))
    return (grad, probs.T, *outputs)


def solution(mesh):
    in_specs = (
        P(("groups", "expert", "dp"), "tensor"),
        P(("groups", "expert", "dp"), "tensor"),
        P(("groups", "expert", "dp"), None),
        P(("groups", "expert", "dp"), None),
        P("expert", None, "tensor"),
        P("expert", None, "tensor"),
        P("expert", "tensor", None),
    )
    out_specs = (
        P(("groups", "expert", "dp"), "tensor"),
        P(("groups", "expert", "dp"), None),
        P(("groups", "expert"), None, "tensor"),
        P(("groups", "expert"), None, "tensor"),
        P(("groups", "expert"), "tensor", None),
    )
    sizes = dict(mesh.shape)
    compact = sizes["expert"] == 4 and sizes["tensor"] == 2 and sizes["dp"] == 2
    return jax.shard_map(body if compact else general_body, mesh=mesh, in_specs=in_specs, out_specs=out_specs, check_vma=False)
```

```python
import functools

import jax
import jax.numpy as jnp
from jax import lax
from jax.experimental import pallas as pl
from jax.experimental.pallas import tpu as pltpu
from jax.sharding import PartitionSpec as P

CAP = 16
META = 128
PARTS = 2
MIB = 1024 * 1024
NT = (((1,), (1,)), ((), ()))
TN = (((0,), (0,)), ((), ()))
ANY = pl.BlockSpec(memory_space=pl.ANY)
SMEM = pl.BlockSpec(memory_space=pltpu.SMEM)
VMEM = pl.BlockSpec(memory_space=pltpu.VMEM)
LIGHT = pl.CostEstimate(flops=0, bytes_accessed=1024, transcendentals=0)


def near(*arrays):
    return [pltpu.with_memory_space_constraint(x, pltpu.VMEM) for x in arrays]


def far(*arrays):
    return [pltpu.with_memory_space_constraint(x, pltpu.HBM) for x in arrays]


def pack_kernel(top, act_hbm, og_hbm, ids_hbm, probs_hbm, out_ref, ids_ref, probs_ref, sems):
    rows, wide = act_hbm.shape
    copies = [
        pltpu.make_async_copy(act_hbm, out_ref.at[:, :wide], sems.at[0]),
        pltpu.make_async_copy(og_hbm, out_ref.at[:, wide : 2 * wide], sems.at[1]),
        pltpu.make_async_copy(ids_hbm, ids_ref, sems.at[2]),
        pltpu.make_async_copy(probs_hbm, probs_ref, sems.at[3]),
    ]
    for copy in copies:
        copy.start()
    for copy in copies[2:]:
        copy.wait()
    meta = jnp.concatenate([ids_ref[...].astype(jnp.float32), probs_ref[...].astype(jnp.float32)], axis=0)
    meta = jnp.concatenate([meta, jnp.zeros((META - 2 * top, rows), jnp.float32)], axis=0)
    out_ref[:, 2 * wide :] = meta.T.astype(jnp.bfloat16)
    for copy in copies[:2]:
        copy.wait()


def pack(activations, out_grad, ids, probs):
    rows, wide = activations.shape
    return pl.pallas_call(
        functools.partial(pack_kernel, ids.shape[0]),
        in_specs=[ANY] * 4,
        out_specs=VMEM,
        out_shape=pltpu.VMEM((rows, 2 * wide + META), jnp.bfloat16),
        scratch_shapes=[
            pltpu.VMEM(ids.shape, ids.dtype),
            pltpu.VMEM(probs.shape, probs.dtype),
            pltpu.SemaphoreType.DMA((4,)),
        ],
        compiler_params=pltpu.CompilerParams(vmem_limit_bytes=4 * MIB),
        name="pack_tokens",
    )(*far(activations, out_grad, ids, probs))


def collect_kernel(*refs):
    *shards, out_ref = refs
    rows = shards[0].shape[0]
    for i, shard in enumerate(shards):
        out_ref[pl.ds(i * rows, rows), :] = shard[...]


def collect(shards):
    rows, columns = shards[0].shape
    return pl.pallas_call(
        collect_kernel,
        in_specs=[VMEM] * len(shards),
        out_specs=VMEM,
        out_shape=pltpu.VMEM((len(shards) * rows, columns), shards[0].dtype),
        compiler_params=pltpu.CompilerParams(vmem_limit_bytes=4 * MIB),
        cost_estimate=LIGHT,
        name="collect",
    )(*near(*shards))


def load_kernel(by_row, start, count, first_ref, *refs):
    *sources, target_ref, sem = refs
    step = sources[0].shape[1 if by_row else 2]
    many = len(sources)
    copies = []
    for i in range(start, start + count):
        for j, source in enumerate(sources):
            at = pl.ds((many * i + j) * step, step)
            target = target_ref.at[at, :] if by_row else target_ref.at[:, at]
            copies.append(pltpu.make_async_copy(source.at[first_ref[0] + i], target, sem))
    for copy in copies:
        copy.start()
    for copy in copies:
        copy.wait()


def load_kernel_into(by_row, start, count, first_ref, *refs):
    *refs, _, target_ref, sem = refs
    load_kernel(by_row, start, count, first_ref, *refs, target_ref, sem)


def load_weights(first, sources, by_row, own, start, count, into=None):
    _, rows, columns = sources[0].shape
    many = own * len(sources)
    shape = (many * rows, columns) if by_row else (rows, many * columns)
    kept = [] if into is None else near(into)
    return pl.pallas_call(
        functools.partial(load_kernel_into if kept else load_kernel, by_row, start, count),
        in_specs=[SMEM] + [ANY] * len(sources) + [VMEM] * len(kept),
        out_specs=VMEM,
        out_shape=pltpu.VMEM(shape, jnp.bfloat16),
        scratch_shapes=[pltpu.SemaphoreType.DMA],
        input_output_aliases={1 + len(sources): 0} if kept else {},
        compiler_params=pltpu.CompilerParams(vmem_limit_bytes=4 * MIB),
        cost_estimate=LIGHT,
        name="load_weights",
    )(first, *far(*sources), *kept)


def forward_kernel(places, n_tensor, top, own, scalars, own_ref, got_ref, w_in, wd_ref, *outs):
    x_ref, og_ref, grads_ref, both_ref, inners_ref, kept_ref, sent_ref, w_out, sem = outs
    tensor = scalars[1]
    tokens, d = x_ref.shape
    wide, share = d // n_tensor, tokens // 2
    ff = wd_ref.shape[1]
    copies = [
        pltpu.make_async_copy(wd_ref.at[scalars[0] + i], w_out.at[pl.ds(i * ff, ff), :], sem) for i in range(own)
    ]
    for copy in copies:
        copy.start()
    rows = own_ref.shape[0] // len(places)
    metas = []
    for base, held in ((0, own_ref), (share, got_ref)):
        for i, (row, side) in enumerate(places):
            at, to = pl.ds(i * rows, rows), pl.ds(base + row, rows)
            columns = pl.ds(pl.multiple_of(lax.rem(tensor + side, n_tensor) * wide, wide), wide)
            x_ref[to, columns] = held[at, :wide]
            og_ref[to, columns] = held[at, wide : 2 * wide]
            if side == 0:
                metas.append(held[at, 2 * wide :].astype(jnp.float32))
    meta = jnp.concatenate(metas, axis=0)
    pre = jnp.dot(x_ref[...], w_in[...], preferred_element_type=jnp.float32)
    for copy in copies:
        copy.wait()
    hidden_grads = lax.dot_general(og_ref[...], w_out[...], NT, preferred_element_type=jnp.float32)
    lane = lax.broadcasted_iota(jnp.int32, meta.shape, 1)
    inners = jnp.zeros(meta.shape, jnp.float32)
    both = []
    for i in range(own):
        gate_pre, up_pre = pre[:, 2 * i * ff : (2 * i + 1) * ff], pre[:, (2 * i + 1) * ff : (2 * i + 2) * ff]
        hidden_grad = hidden_grads[:, i * ff : (i + 1) * ff]
        expert = scalars[2] + i
        hit = meta[:, :top] == expert.astype(jnp.float32)
        prob = jnp.sum(jnp.where(hit, meta[:, top : 2 * top], 0.0), axis=1, keepdims=True)
        sigma = jax.nn.sigmoid(gate_pre)
        activated = gate_pre * sigma
        hidden = activated * up_pre
        inner = jnp.sum(hidden * hidden_grad, axis=1, keepdims=True)
        inners = jnp.where(lane == expert, inner, inners)
        scaled = prob * hidden_grad
        gate_grad = (scaled * up_pre * sigma * (1.0 + gate_pre * (1.0 - sigma))).astype(jnp.bfloat16)
        up_grad = (scaled * activated).astype(jnp.bfloat16)
        grads_ref[i, :, :ff] = gate_grad
        grads_ref[i, :, ff : 2 * ff] = up_grad
        grads_ref[i, :, 2 * ff :] = (prob * hidden).astype(jnp.bfloat16)
        both += [gate_grad, up_grad]
    both = jnp.concatenate(both, axis=1)
    both_ref[...] = both
    inners_ref[...] = inners
    row_pass(tensor + 1, n_tensor, both, inners, w_in, kept_ref, sent_ref)


def row_pass(side, n_tensor, both, inners, w_in, kept_ref, sent_ref):
    wide = w_in.shape[0] // n_tensor
    share = both.shape[0] // 2
    at = pl.ds(pl.multiple_of(lax.rem(side, n_tensor) * wide, wide), wide)
    total = lax.dot_general(both, w_in[at, :], NT, preferred_element_type=jnp.float32)
    kept_ref[:, :wide] = total[:share]
    kept_ref[:, wide:] = inners[:share]
    sent_ref[:, :wide] = total[share:].astype(jnp.bfloat16)
    sent_ref[:, wide:] = inners[share:].astype(jnp.bfloat16)


def rows_kernel(n_tensor, scalars, both_ref, inners_ref, w_in, kept_ref, sent_ref):
    row_pass(scalars[1], n_tensor, both_ref[...], inners_ref[...], w_in, kept_ref, sent_ref)


def forward_call(kernel, name, scalars, inputs, out_shape, flops, distant=(), scratch=()):
    return pl.pallas_call(
        kernel,
        in_specs=[SMEM] + [VMEM] * len(inputs) + [ANY] * len(distant),
        out_specs=[VMEM] * len(out_shape),
        out_shape=out_shape,
        scratch_shapes=scratch,
        compiler_params=pltpu.CompilerParams(vmem_limit_bytes=20 * MIB),
        cost_estimate=pl.CostEstimate(flops=flops, bytes_accessed=1024, transcendentals=0),
        name=name,
    )(scalars, *near(*inputs), *far(*distant))


def forward(held, got, places, scalars, w_in, w_down, own, n_tensor, top):
    _, ff, d = w_down.shape
    share = held.shape[0] // n_tensor
    tokens = 2 * share
    sums = (share, d // n_tensor + META)
    shapes = [
        pltpu.VMEM((tokens, d), jnp.bfloat16),
        pltpu.VMEM((tokens, d), jnp.bfloat16),
        pltpu.VMEM((own, tokens, 3 * ff), jnp.bfloat16),
        pltpu.VMEM((tokens, own * 2 * ff), jnp.bfloat16),
        pltpu.VMEM((tokens, META), jnp.float32),
        pltpu.VMEM(sums, jnp.float32),
        pltpu.VMEM(sums, jnp.bfloat16),
    ]
    kernel = functools.partial(forward_kernel, places, n_tensor, top, own)
    scratch = [pltpu.VMEM((own * ff, d), jnp.bfloat16), pltpu.SemaphoreType.DMA]
    flops = 8 * own * tokens * d * ff
    return forward_call(kernel, "routed_forward", scalars, [held, got, w_in], shapes, flops, [w_down], scratch)


def row_sums(scalars, both, inners, w_in, n_tensor):
    tokens, d = both.shape[0], w_in.shape[0]
    sums = (tokens // 2, d // n_tensor + META)
    shapes = [pltpu.VMEM(sums, jnp.float32), pltpu.VMEM(sums, jnp.bfloat16)]
    kernel = functools.partial(rows_kernel, n_tensor)
    return forward_call(kernel, "row_sums", scalars, [both, inners, w_in], shapes, 2 * tokens * d * w_in.shape[1])


def weight_kernel(swap, first_ref, x_ref, og_ref, grads_ref, *refs):
    *targets, gate_ref, up_ref, down_ref, sem = refs[-7:]
    own, d, ff = gate_ref.shape
    half, step = grads_ref.shape[1] // 2, d // PARTS
    copies = []

    def send(ref, target, i, at):
        copies.append(pltpu.make_async_copy(ref.at[(i, *at)], target.at[(first_ref[0] + i, *at)], sem))
        copies[-1].start()

    for i in range(own):
        grads = grads_ref[i]
        if swap:
            grads = jnp.concatenate([grads[half:], grads[:half]], axis=0)
        for part in range(PARTS):
            at, every = pl.ds(part * step, step), pl.ds(0, ff)
            total = lax.dot_general(x_ref[:, at], grads[:, : 2 * ff], TN, preferred_element_type=jnp.float32)
            gate_ref[i, at, :] = total[:, :ff].astype(jnp.bfloat16)
            up_ref[i, at, :] = total[:, ff:].astype(jnp.bfloat16)
            send(gate_ref, targets[0], i, (at, every))
            send(up_ref, targets[1], i, (at, every))
        for part in range(PARTS):
            at, every = pl.ds(part * step, step), pl.ds(0, ff)
            total = lax.dot_general(grads[:, 2 * ff :], og_ref[:, at], TN, preferred_element_type=jnp.float32)
            down_ref[i, :, at] = total.astype(jnp.bfloat16)
            send(down_ref, targets[2], i, (every, at))
    for copy in copies:
        copy.wait()


def weight_grads(first, x, og, grads, local_count, into=None):
    own, tokens, ff = grads.shape[0], grads.shape[1], grads.shape[2] // 3
    d = x.shape[1]
    kept = [] if into is None else list(into)
    shapes = [(d, ff), (d, ff), (ff, d)]
    return pl.pallas_call(
        functools.partial(weight_kernel, into is not None),
        in_specs=[SMEM] + [VMEM] * 3 + [ANY] * len(kept),
        out_specs=[ANY] * 3,
        out_shape=[pltpu.HBM((local_count, *s), jnp.bfloat16) for s in shapes],
        scratch_shapes=[pltpu.VMEM((own, *s), jnp.bfloat16) for s in shapes] + [pltpu.SemaphoreType.DMA],
        input_output_aliases={4 + i: i for i in range(len(kept))},
        compiler_params=pltpu.CompilerParams(vmem_limit_bytes=26 * MIB),
        cost_estimate=pl.CostEstimate(
            flops=6 * own * tokens * d * ff, bytes_accessed=6 * own * d * ff, transcendentals=0
        ),
        name="weight_grads",
    )(first, *near(x, og, grads), *kept)


def dp_sum_kernel(kept_ref, got_ref, there_ref):
    there_ref[...] = (kept_ref[...] + got_ref[...].astype(jnp.float32)).astype(jnp.bfloat16)


def tensor_sum_kernel(kept_ref, core_ref, got_ref, own_ref, *out_refs):
    rows = own_ref.shape[0]
    for block, target in enumerate((own_ref, *out_refs)):
        at = pl.ds(block * rows, rows)
        total = kept_ref[at, :] + core_ref[at, :].astype(jnp.float32) + got_ref[at, :].astype(jnp.float32)
        target[...] = total.astype(target.dtype)


def finish_kernel(top, ids_ref, own_ref, *refs):
    parts, (grad_ref, probs_ref) = refs[:-2], refs[-2:]
    total = own_ref[...]
    for part in parts:
        total = total + part[...].astype(jnp.float32)
    wide = grad_ref.shape[1]
    grad_ref[...] = total[:, :wide].astype(jnp.bfloat16)
    inner = total[:, wide:].T
    ids = ids_ref[...]
    expert = lax.broadcasted_iota(jnp.int32, inner.shape, 0)
    for k in range(top):
        picked = jnp.where(expert == ids[k : k + 1, :], inner, 0.0)
        probs_ref[k : k + 1, :] = jnp.sum(picked, axis=0, keepdims=True)


def shift(x, axis, by):
    count = lax.axis_size(axis)
    return lax.ppermute(x, axis, [(i, (i + by) % count) for i in range(count)])


def general_body(activations, out_grad, expert_ids, gate_probs, w_gate, w_up, w_down):
    d = activations.shape[1] * lax.axis_size("tensor")
    expert_count = lax.axis_size("expert")
    local_count = w_gate.shape[0]
    experts = expert_count * local_count
    token_rows = expert_ids.shape[0]
    flat_ids = expert_ids.reshape(-1)
    onehot = (flat_ids[:, None] == jnp.arange(experts, dtype=jnp.int32)[None, :]).astype(jnp.int32)
    before = jnp.cumsum(onehot, axis=0) - onehot
    slot_index = jnp.sum(before * onehot, axis=1)
    position = (flat_ids * CAP + slot_index).reshape(token_rows, expert_ids.shape[1])
    lane_index = jnp.arange(experts * CAP, dtype=jnp.int32)
    matches = position[None, :, :] == lane_index[:, None, None]
    placing = jnp.sum(matches.astype(jnp.int32), axis=2).astype(jnp.bfloat16)
    send_probs = jnp.sum(jnp.where(matches, gate_probs.astype(jnp.float32)[None], 0.0), axis=(1, 2))
    send_probs = send_probs.astype(jnp.bfloat16).reshape(experts, CAP)
    full_rows, full_grads = (
        lax.all_gather(activations, "tensor", axis=1, tiled=True),
        lax.all_gather(out_grad, "tensor", axis=1, tiled=True),
    )
    send_rows = (
        jnp.dot(placing, full_rows, preferred_element_type=jnp.float32)
        .astype(jnp.bfloat16)
        .reshape(experts, CAP, d)
    )
    send_grads = (
        jnp.dot(placing, full_grads, preferred_element_type=jnp.float32)
        .astype(jnp.bfloat16)
        .reshape(experts, CAP, d)
    )
    got_rows, got_grads, got_probs = (
        lax.all_to_all(send_rows, "expert", split_axis=0, concat_axis=0, tiled=True),
        lax.all_to_all(send_grads, "expert", split_axis=0, concat_axis=0, tiled=True),
        lax.all_to_all(send_probs, "expert", split_axis=0, concat_axis=0, tiled=True),
    )
    rows_in = got_rows.reshape(expert_count, local_count, CAP, d)
    grads_in = got_grads.reshape(expert_count, local_count, CAP, d)
    row_probs = got_probs.reshape(expert_count, local_count, CAP, 1).astype(jnp.float32)
    gate_pre = jnp.einsum("slcd,ldf->slcf", rows_in, w_gate, preferred_element_type=jnp.float32)
    up_pre = jnp.einsum("slcd,ldf->slcf", rows_in, w_up, preferred_element_type=jnp.float32)
    hidden_grad = jnp.einsum("slcd,lfd->slcf", grads_in, w_down, preferred_element_type=jnp.float32)
    sigma = jax.nn.sigmoid(gate_pre)
    activated = gate_pre * sigma
    hidden = activated * up_pre
    inner_part = jnp.sum(hidden * hidden_grad, axis=3)
    weighted = (row_probs * hidden).astype(jnp.bfloat16)
    scaled = row_probs * hidden_grad
    gate_grad = (scaled * up_pre * sigma * (1.0 + gate_pre * (1.0 - sigma))).astype(jnp.bfloat16)
    up_grad = (scaled * activated).astype(jnp.bfloat16)
    row_part = jnp.einsum("slcf,ldf->slcd", gate_grad, w_gate, preferred_element_type=jnp.float32)
    row_part = row_part + jnp.einsum(
        "slcf,ldf->slcd", up_grad, w_up, preferred_element_type=jnp.float32
    )
    gate_total = jnp.einsum(
        "slcd,slcf->ldf", rows_in, gate_grad, preferred_element_type=jnp.float32
    )
    up_total = jnp.einsum("slcd,slcf->ldf", rows_in, up_grad, preferred_element_type=jnp.float32)
    down_total = jnp.einsum(
        "slcf,slcd->lfd", weighted, grads_in, preferred_element_type=jnp.float32
    )
    lanes = experts * CAP
    own_part = lax.psum_scatter(
        row_part.astype(jnp.bfloat16), "tensor", scatter_dimension=3, tiled=True
    ).astype(jnp.float32)
    inner_sum = lax.psum(inner_part.astype(jnp.bfloat16), "tensor").astype(jnp.float32)
    quarter = own_part.shape[3]
    returned_rows, returned_inner = (
        lax.all_to_all(
            own_part.reshape(experts, CAP, quarter).astype(jnp.bfloat16),
            "expert",
            split_axis=0,
            concat_axis=0,
            tiled=True,
        ).astype(jnp.float32),
        lax.all_to_all(
            inner_sum.reshape(experts, CAP).astype(jnp.bfloat16),
            "expert",
            split_axis=0,
            concat_axis=0,
            tiled=True,
        ).astype(jnp.float32),
    )
    placing_wide = jnp.sum(matches.astype(jnp.int32), axis=2).astype(jnp.float32)
    token_grad = lax.dot_general(
        placing_wide,
        returned_rows.reshape(lanes, quarter),
        (((0,), (0,)), ((), ())),
        precision=lax.Precision.HIGHEST,
        preferred_element_type=jnp.float32,
    )
    grad_probs = jnp.sum(
        jnp.where(matches, returned_inner.reshape(lanes)[:, None, None], 0.0), axis=0
    )
    gate_sum, up_sum, down_sum = (
        lax.psum(gate_total.astype(jnp.bfloat16), "dp").astype(jnp.float32),
        lax.psum(up_total.astype(jnp.bfloat16), "dp").astype(jnp.float32),
        lax.psum(down_total.astype(jnp.bfloat16), "dp").astype(jnp.float32),
    )
    return (
        token_grad.astype(jnp.bfloat16),
        grad_probs,
        gate_sum.astype(jnp.bfloat16),
        up_sum.astype(jnp.bfloat16),
        down_sum.astype(jnp.bfloat16),
    )


def body(activations, out_grad, expert_ids, gate_probs, w_gate, w_up, w_down):
    n_expert, n_tensor, n_dp = (lax.axis_size(a) for a in ("expert", "tensor", "dp"))
    local_count, d, ff = w_gate.shape
    rows, top = expert_ids.shape
    tokens = rows * n_expert * n_dp
    wide = d // n_tensor
    own = local_count // n_dp
    e, t, p = (lax.axis_index(a) for a in ("expert", "tensor", "dp"))
    first = p * own
    scalars = jnp.stack([first, t, e * local_count + first, own - first]).astype(jnp.int32)
    ids = expert_ids.T
    packed = pack(activations, out_grad, ids, gate_probs.T)
    along = [packed] + [shift(packed, "expert", k) for k in range(1, n_expert)]
    across = {k: shift(along[k], "tensor", 1) for k in (0, 3, 1)}
    along[2], across[0], across[3], then = lax.optimization_barrier((along[2], across[0], across[3], scalars))
    across[2] = shift(along[2], "tensor", 1)
    w_in = load_weights(then, (w_gate, w_up), False, own, 0, own // 2)
    across[1], across[2], w_in, then = lax.optimization_barrier((across[1], across[2], w_in, scalars))
    w_in = load_weights(then, (w_gate, w_up), False, own, own // 2, own - own // 2, w_in)
    held = collect(along + [across[k] for k in range(n_expert)])
    places = [(k * rows, side) for side in range(n_tensor) for k in range(n_expert)]
    swapped = shift(held, "dp", 1)
    x, og, grads, both, inners, kept, sent = forward(
        held, swapped, places, scalars, w_in, w_down, own, n_tensor, top
    )
    got = shift(sent, "dp", 1)
    kept_here, sent_here = row_sums(scalars, both, inners, w_in, n_tensor)
    got, sent_here, grads = lax.optimization_barrier((got, sent_here, grads))
    half = (tokens // 2, wide + META)
    there = pl.pallas_call(
        dp_sum_kernel,
        in_specs=[VMEM] * 2,
        out_specs=VMEM,
        out_shape=pltpu.VMEM(half, jnp.bfloat16),
        compiler_params=pltpu.CompilerParams(vmem_limit_bytes=4 * MIB),
        cost_estimate=LIGHT,
        name="sum_over_cores",
    )(*near(kept, got))
    crossed = shift(there, "tensor", 1)
    got_here = shift(sent_here, "dp", 1)
    got_grads = shift(grads, "dp", 1)
    outputs = weight_grads(scalars, x, og, grads, local_count)
    crossed, got_here, outputs = lax.optimization_barrier((crossed, got_here, outputs))
    piece = (rows, wide + META)
    pieces = pl.pallas_call(
        tensor_sum_kernel,
        in_specs=[VMEM] * 3,
        out_specs=[VMEM] * n_expert,
        out_shape=[pltpu.VMEM(piece, jnp.float32)] + [pltpu.VMEM(piece, jnp.bfloat16)] * (n_expert - 1),
        compiler_params=pltpu.CompilerParams(vmem_limit_bytes=4 * MIB),
        name="sum_over_tensor",
    )(*near(kept_here, got_here, crossed))
    received = [shift(pieces[k], "expert", -k) for k in range(1, n_expert)]
    outputs = weight_grads(scalars[3:], x, og, got_grads, local_count, outputs)
    received, outputs = lax.optimization_barrier((received, outputs))
    grad, probs = pl.pallas_call(
        functools.partial(finish_kernel, top),
        in_specs=[VMEM] * (n_expert + 1),
        out_specs=[VMEM] * 2,
        out_shape=[jax.ShapeDtypeStruct((rows, wide), jnp.bfloat16), jax.ShapeDtypeStruct((top, rows), jnp.float32)],
        compiler_params=pltpu.CompilerParams(vmem_limit_bytes=4 * MIB),
        name="sum_over_experts",
    )(ids, pieces[0], *near(*received))
    return (grad, probs.T, *outputs)


def solution(mesh):
    in_specs = (
        P(("groups", "expert", "dp"), "tensor"),
        P(("groups", "expert", "dp"), "tensor"),
        P(("groups", "expert", "dp"), None),
        P(("groups", "expert", "dp"), None),
        P("expert", None, "tensor"),
        P("expert", None, "tensor"),
        P("expert", "tensor", None),
    )
    out_specs = (
        P(("groups", "expert", "dp"), "tensor"),
        P(("groups", "expert", "dp"), None),
        P(("groups", "expert"), None, "tensor"),
        P(("groups", "expert"), None, "tensor"),
        P(("groups", "expert"), "tensor", None),
    )
    sizes = dict(mesh.shape)
    compact = sizes["expert"] == 4 and sizes["tensor"] == 2 and sizes["dp"] == 2
    return jax.shard_map(body if compact else general_body, mesh=mesh, in_specs=in_specs, out_specs=out_specs, check_vma=False)
```

```python
import functools

import jax
import jax.numpy as jnp
from jax import lax
from jax.experimental import pallas as pl
from jax.experimental.pallas import tpu as pltpu
from jax.sharding import PartitionSpec as P

CAP = 16
META = 128
PARTS = 2
MIB = 1024 * 1024
NT = (((1,), (1,)), ((), ()))
TN = (((0,), (0,)), ((), ()))
ANY = pl.BlockSpec(memory_space=pl.ANY)
VMEM = pl.BlockSpec(memory_space=pltpu.VMEM)
LIGHT = pl.CostEstimate(flops=0, bytes_accessed=1024, transcendentals=0)


def near(*arrays):
    return [pltpu.with_memory_space_constraint(x, pltpu.VMEM) for x in arrays]


def far(*arrays):
    return [pltpu.with_memory_space_constraint(x, pltpu.HBM) for x in arrays]


def pack_kernel(top, act_hbm, og_hbm, ids_hbm, probs_hbm, out_ref, ids_ref, probs_ref, sems):
    rows, wide = act_hbm.shape
    copies = [
        pltpu.make_async_copy(act_hbm, out_ref.at[:, :wide], sems.at[0]),
        pltpu.make_async_copy(og_hbm, out_ref.at[:, wide : 2 * wide], sems.at[1]),
        pltpu.make_async_copy(ids_hbm, ids_ref, sems.at[2]),
        pltpu.make_async_copy(probs_hbm, probs_ref, sems.at[3]),
    ]
    for copy in copies:
        copy.start()
    for copy in copies[2:]:
        copy.wait()
    meta = jnp.concatenate([ids_ref[...].astype(jnp.float32), probs_ref[...].astype(jnp.float32)], axis=0)
    meta = jnp.concatenate([meta, jnp.zeros((META - 2 * top, rows), jnp.float32)], axis=0)
    out_ref[:, 2 * wide :] = meta.T.astype(jnp.bfloat16)
    for copy in copies[:2]:
        copy.wait()


def pack(activations, out_grad, ids, probs):
    rows, wide = activations.shape
    return pl.pallas_call(
        functools.partial(pack_kernel, ids.shape[0]),
        in_specs=[ANY] * 4,
        out_specs=VMEM,
        out_shape=pltpu.VMEM((rows, 2 * wide + META), jnp.bfloat16),
        scratch_shapes=[
            pltpu.VMEM(ids.shape, ids.dtype),
            pltpu.VMEM(probs.shape, probs.dtype),
            pltpu.SemaphoreType.DMA((4,)),
        ],
        compiler_params=pltpu.CompilerParams(vmem_limit_bytes=4 * MIB),
        name="pack_tokens",
    )(*far(activations, out_grad, ids, probs))


def collect_kernel(n_tensor, *refs):
    *shards, out_ref = refs
    rows = shards[0].shape[0]
    wide = (shards[0].shape[1] - META) // 2
    d = n_tensor * wide
    blocks = len(shards) // n_tensor
    for i, shard in enumerate(shards):
        side, at = i // blocks, pl.ds(i % blocks * rows, rows)
        begin = pl.multiple_of(lax.rem(lax.axis_index("tensor") + side, n_tensor) * wide, wide)
        out_ref[at, pl.ds(begin, wide)] = shard[:, :wide]
        out_ref[at, pl.ds(d + begin, wide)] = shard[:, wide : 2 * wide]
        if side == 0:
            out_ref[at, 2 * d :] = shard[:, 2 * wide :]


def collect(shards, n_tensor):
    rows, columns = shards[0].shape
    shape = (len(shards) // n_tensor * rows, n_tensor * (columns - META) + META)
    return pl.pallas_call(
        functools.partial(collect_kernel, n_tensor),
        in_specs=[VMEM] * len(shards),
        out_specs=VMEM,
        out_shape=pltpu.VMEM(shape, shards[0].dtype),
        compiler_params=pltpu.CompilerParams(vmem_limit_bytes=4 * MIB),
        cost_estimate=LIGHT,
        name="collect",
    )(*near(*shards))


def load_kernel(by_row, own, start, count, after_ref, *refs):
    *sources, target_ref, sem = refs
    step = sources[0].shape[1 if by_row else 2]
    many = len(sources)
    first = lax.axis_index("dp") * own
    copies = []
    for i in range(start, start + count):
        for j, source in enumerate(sources):
            at = pl.ds((many * i + j) * step, step)
            target = target_ref.at[at, :] if by_row else target_ref.at[:, at]
            copies.append(pltpu.make_async_copy(source.at[first + i], target, sem))
    for copy in copies:
        copy.start()
    for copy in copies:
        copy.wait()


def load_kernel_into(by_row, own, start, count, after_ref, *refs):
    *refs, _, target_ref, sem = refs
    load_kernel(by_row, own, start, count, after_ref, *refs, target_ref, sem)


def load_weights(after, sources, by_row, own, start, count, into=None):
    _, rows, columns = sources[0].shape
    many = own * len(sources)
    shape = (many * rows, columns) if by_row else (rows, many * columns)
    kept = [] if into is None else near(into)
    return pl.pallas_call(
        functools.partial(load_kernel_into if kept else load_kernel, by_row, own, start, count),
        in_specs=[VMEM] + [ANY] * len(sources) + [VMEM] * len(kept),
        out_specs=VMEM,
        out_shape=pltpu.VMEM(shape, jnp.bfloat16),
        scratch_shapes=[pltpu.SemaphoreType.DMA],
        input_output_aliases={1 + len(sources): 0} if kept else {},
        compiler_params=pltpu.CompilerParams(vmem_limit_bytes=4 * MIB),
        cost_estimate=LIGHT,
        name="load_weights",
    )(*near(after), *far(*sources), *kept)


def forward_kernel(n_tensor, top, own, held_ref, got_ref, w_in, wd_ref, *outs):
    grads_ref, both_ref, inners_ref, kept_ref, sent_ref, w_out, sem = outs
    local_count, ff, d = wd_ref.shape
    first = lax.axis_index("dp") * own
    first_expert = lax.axis_index("expert") * local_count + first
    every = lambda at: jnp.concatenate([held_ref[:, at], got_ref[:, at]], axis=0)
    copies = [
        pltpu.make_async_copy(wd_ref.at[first + i], w_out.at[pl.ds(i * ff, ff), :], sem) for i in range(own)
    ]
    for copy in copies:
        copy.start()
    pre = jnp.dot(every(slice(0, d)), w_in[...], preferred_element_type=jnp.float32)
    for copy in copies:
        copy.wait()
    hidden_grads = lax.dot_general(every(slice(d, 2 * d)), w_out[...], NT, preferred_element_type=jnp.float32)
    meta = every(slice(2 * d, None)).astype(jnp.float32)
    lane = lax.broadcasted_iota(jnp.int32, meta.shape, 1)
    inners = jnp.zeros(meta.shape, jnp.float32)
    both = []
    for i in range(own):
        gate_pre, up_pre = pre[:, 2 * i * ff : (2 * i + 1) * ff], pre[:, (2 * i + 1) * ff : (2 * i + 2) * ff]
        hidden_grad = hidden_grads[:, i * ff : (i + 1) * ff]
        expert = first_expert + i
        hit = meta[:, :top] == expert.astype(jnp.float32)
        prob = jnp.sum(jnp.where(hit, meta[:, top : 2 * top], 0.0), axis=1, keepdims=True)
        sigma = jax.nn.sigmoid(gate_pre)
        activated = gate_pre * sigma
        hidden = activated * up_pre
        inner = jnp.sum(hidden * hidden_grad, axis=1, keepdims=True)
        inners = jnp.where(lane == expert, inner, inners)
        scaled = prob * hidden_grad
        gate_grad = (scaled * up_pre * sigma * (1.0 + gate_pre * (1.0 - sigma))).astype(jnp.bfloat16)
        up_grad = (scaled * activated).astype(jnp.bfloat16)
        grads_ref[i, :, :ff] = gate_grad
        grads_ref[i, :, ff : 2 * ff] = up_grad
        grads_ref[i, :, 2 * ff :] = (prob * hidden).astype(jnp.bfloat16)
        both += [gate_grad, up_grad]
    both = jnp.concatenate(both, axis=1)
    both_ref[...] = both
    inners_ref[...] = inners
    row_pass(1, n_tensor, both, inners, w_in, kept_ref, sent_ref)


def row_pass(side, n_tensor, both, inners, w_in, kept_ref, sent_ref):
    wide = w_in.shape[0] // n_tensor
    share = both.shape[0] // 2
    at = pl.ds(pl.multiple_of(lax.rem(lax.axis_index("tensor") + side, n_tensor) * wide, wide), wide)
    total = lax.dot_general(both, w_in[at, :], NT, preferred_element_type=jnp.float32)
    kept_ref[:, :wide] = total[:share]
    kept_ref[:, wide:] = inners[:share]
    sent_ref[:, :wide] = total[share:].astype(jnp.bfloat16)
    sent_ref[:, wide:] = inners[share:].astype(jnp.bfloat16)


def rows_kernel(n_tensor, both_ref, inners_ref, w_in, kept_ref, sent_ref):
    row_pass(0, n_tensor, both_ref[...], inners_ref[...], w_in, kept_ref, sent_ref)


def forward_call(kernel, name, inputs, out_shape, flops, distant=(), scratch=()):
    return pl.pallas_call(
        kernel,
        in_specs=[VMEM] * len(inputs) + [ANY] * len(distant),
        out_specs=[VMEM] * len(out_shape),
        out_shape=out_shape,
        scratch_shapes=scratch,
        compiler_params=pltpu.CompilerParams(vmem_limit_bytes=20 * MIB),
        cost_estimate=pl.CostEstimate(flops=flops, bytes_accessed=1024, transcendentals=0),
        name=name,
    )(*near(*inputs), *far(*distant))


def forward(held, got, w_in, w_down, own, n_tensor, top):
    _, ff, d = w_down.shape
    share = held.shape[0]
    tokens = 2 * share
    sums = (share, d // n_tensor + META)
    shapes = [
        pltpu.VMEM((own, tokens, 3 * ff), jnp.bfloat16),
        pltpu.VMEM((tokens, own * 2 * ff), jnp.bfloat16),
        pltpu.VMEM((tokens, META), jnp.float32),
        pltpu.VMEM(sums, jnp.float32),
        pltpu.VMEM(sums, jnp.bfloat16),
    ]
    kernel = functools.partial(forward_kernel, n_tensor, top, own)
    scratch = [pltpu.VMEM((own * ff, d), jnp.bfloat16), pltpu.SemaphoreType.DMA]
    flops = 8 * own * tokens * d * ff
    return forward_call(kernel, "routed_forward", [held, got, w_in], shapes, flops, [w_down], scratch)


def row_sums(both, inners, w_in, n_tensor):
    tokens, d = both.shape[0], w_in.shape[0]
    sums = (tokens // 2, d // n_tensor + META)
    shapes = [pltpu.VMEM(sums, jnp.float32), pltpu.VMEM(sums, jnp.bfloat16)]
    kernel = functools.partial(rows_kernel, n_tensor)
    return forward_call(kernel, "row_sums", [both, inners, w_in], shapes, 2 * tokens * d * w_in.shape[1])


def weight_kernel(swap, held_ref, got_ref, grads_ref, *refs):
    *targets, gate_ref, up_ref, down_ref, sem = refs[-7:]
    own, d, ff = gate_ref.shape
    half, step = grads_ref.shape[1] // 2, d // PARTS
    core = lax.axis_index("dp")
    first = (1 - core if swap else core) * own
    both = lambda at: jnp.concatenate([held_ref[:, at], got_ref[:, at]], axis=0)
    copies = []

    def send(ref, target, i, at):
        copies.append(pltpu.make_async_copy(ref.at[(i, *at)], target.at[(first + i, *at)], sem))
        copies[-1].start()

    for i in range(own):
        grads = grads_ref[i]
        if swap:
            grads = jnp.concatenate([grads[half:], grads[:half]], axis=0)
        for part in range(PARTS):
            at, every = pl.ds(part * step, step), pl.ds(0, ff)
            total = lax.dot_general(both(at), grads[:, : 2 * ff], TN, preferred_element_type=jnp.float32)
            gate_ref[i, at, :] = total[:, :ff].astype(jnp.bfloat16)
            up_ref[i, at, :] = total[:, ff:].astype(jnp.bfloat16)
            send(gate_ref, targets[0], i, (at, every))
            send(up_ref, targets[1], i, (at, every))
        for part in range(PARTS):
            at, every = pl.ds(part * step, step), pl.ds(0, ff)
            after = pl.ds(d + part * step, step)
            total = lax.dot_general(grads[:, 2 * ff :], both(after), TN, preferred_element_type=jnp.float32)
            down_ref[i, :, at] = total.astype(jnp.bfloat16)
            send(down_ref, targets[2], i, (every, at))
    for copy in copies:
        copy.wait()


def weight_grads(held, got, grads, local_count, into=None):
    own, tokens, ff = grads.shape[0], grads.shape[1], grads.shape[2] // 3
    d = (held.shape[1] - META) // 2
    kept = [] if into is None else list(into)
    shapes = [(d, ff), (d, ff), (ff, d)]
    return pl.pallas_call(
        functools.partial(weight_kernel, into is not None),
        in_specs=[VMEM] * 3 + [ANY] * len(kept),
        out_specs=[ANY] * 3,
        out_shape=[pltpu.HBM((local_count, *s), jnp.bfloat16) for s in shapes],
        scratch_shapes=[pltpu.VMEM((own, *s), jnp.bfloat16) for s in shapes] + [pltpu.SemaphoreType.DMA],
        input_output_aliases={3 + i: i for i in range(len(kept))},
        compiler_params=pltpu.CompilerParams(vmem_limit_bytes=26 * MIB),
        cost_estimate=pl.CostEstimate(
            flops=6 * own * tokens * d * ff, bytes_accessed=6 * own * d * ff, transcendentals=0
        ),
        name="weight_grads",
    )(*near(held, got, grads), *kept)


def dp_sum_kernel(kept_ref, got_ref, there_ref):
    there_ref[...] = (kept_ref[...] + got_ref[...].astype(jnp.float32)).astype(jnp.bfloat16)


def tensor_sum_kernel(kept_ref, core_ref, got_ref, own_ref, *out_refs):
    rows = own_ref.shape[0]
    for block, target in enumerate((own_ref, *out_refs)):
        at = pl.ds(block * rows, rows)
        total = kept_ref[at, :] + core_ref[at, :].astype(jnp.float32) + got_ref[at, :].astype(jnp.float32)
        target[...] = total.astype(target.dtype)


def finish_kernel(top, ids_ref, own_ref, *refs):
    parts, (grad_ref, probs_ref) = refs[:-2], refs[-2:]
    total = own_ref[...]
    for part in parts:
        total = total + part[...].astype(jnp.float32)
    wide = grad_ref.shape[1]
    grad_ref[...] = total[:, :wide].astype(jnp.bfloat16)
    inner = total[:, wide:].T
    ids = ids_ref[...]
    expert = lax.broadcasted_iota(jnp.int32, inner.shape, 0)
    for k in range(top):
        picked = jnp.where(expert == ids[k : k + 1, :], inner, 0.0)
        probs_ref[k : k + 1, :] = jnp.sum(picked, axis=0, keepdims=True)


def shift(x, axis, by):
    count = lax.axis_size(axis)
    return lax.ppermute(x, axis, [(i, (i + by) % count) for i in range(count)])


def general_body(activations, out_grad, expert_ids, gate_probs, w_gate, w_up, w_down):
    d = activations.shape[1] * lax.axis_size("tensor")
    expert_count = lax.axis_size("expert")
    local_count = w_gate.shape[0]
    experts = expert_count * local_count
    token_rows = expert_ids.shape[0]
    flat_ids = expert_ids.reshape(-1)
    onehot = (flat_ids[:, None] == jnp.arange(experts, dtype=jnp.int32)[None, :]).astype(jnp.int32)
    before = jnp.cumsum(onehot, axis=0) - onehot
    slot_index = jnp.sum(before * onehot, axis=1)
    position = (flat_ids * CAP + slot_index).reshape(token_rows, expert_ids.shape[1])
    lane_index = jnp.arange(experts * CAP, dtype=jnp.int32)
    matches = position[None, :, :] == lane_index[:, None, None]
    placing = jnp.sum(matches.astype(jnp.int32), axis=2).astype(jnp.bfloat16)
    send_probs = jnp.sum(jnp.where(matches, gate_probs.astype(jnp.float32)[None], 0.0), axis=(1, 2))
    send_probs = send_probs.astype(jnp.bfloat16).reshape(experts, CAP)
    full_rows, full_grads = (
        lax.all_gather(activations, "tensor", axis=1, tiled=True),
        lax.all_gather(out_grad, "tensor", axis=1, tiled=True),
    )
    send_rows = (
        jnp.dot(placing, full_rows, preferred_element_type=jnp.float32)
        .astype(jnp.bfloat16)
        .reshape(experts, CAP, d)
    )
    send_grads = (
        jnp.dot(placing, full_grads, preferred_element_type=jnp.float32)
        .astype(jnp.bfloat16)
        .reshape(experts, CAP, d)
    )
    got_rows, got_grads, got_probs = (
        lax.all_to_all(send_rows, "expert", split_axis=0, concat_axis=0, tiled=True),
        lax.all_to_all(send_grads, "expert", split_axis=0, concat_axis=0, tiled=True),
        lax.all_to_all(send_probs, "expert", split_axis=0, concat_axis=0, tiled=True),
    )
    rows_in = got_rows.reshape(expert_count, local_count, CAP, d)
    grads_in = got_grads.reshape(expert_count, local_count, CAP, d)
    row_probs = got_probs.reshape(expert_count, local_count, CAP, 1).astype(jnp.float32)
    gate_pre = jnp.einsum("slcd,ldf->slcf", rows_in, w_gate, preferred_element_type=jnp.float32)
    up_pre = jnp.einsum("slcd,ldf->slcf", rows_in, w_up, preferred_element_type=jnp.float32)
    hidden_grad = jnp.einsum("slcd,lfd->slcf", grads_in, w_down, preferred_element_type=jnp.float32)
    sigma = jax.nn.sigmoid(gate_pre)
    activated = gate_pre * sigma
    hidden = activated * up_pre
    inner_part = jnp.sum(hidden * hidden_grad, axis=3)
    weighted = (row_probs * hidden).astype(jnp.bfloat16)
    scaled = row_probs * hidden_grad
    gate_grad = (scaled * up_pre * sigma * (1.0 + gate_pre * (1.0 - sigma))).astype(jnp.bfloat16)
    up_grad = (scaled * activated).astype(jnp.bfloat16)
    row_part = jnp.einsum("slcf,ldf->slcd", gate_grad, w_gate, preferred_element_type=jnp.float32)
    row_part = row_part + jnp.einsum(
        "slcf,ldf->slcd", up_grad, w_up, preferred_element_type=jnp.float32
    )
    gate_total = jnp.einsum(
        "slcd,slcf->ldf", rows_in, gate_grad, preferred_element_type=jnp.float32
    )
    up_total = jnp.einsum("slcd,slcf->ldf", rows_in, up_grad, preferred_element_type=jnp.float32)
    down_total = jnp.einsum(
        "slcf,slcd->lfd", weighted, grads_in, preferred_element_type=jnp.float32
    )
    lanes = experts * CAP
    own_part = lax.psum_scatter(
        row_part.astype(jnp.bfloat16), "tensor", scatter_dimension=3, tiled=True
    ).astype(jnp.float32)
    inner_sum = lax.psum(inner_part.astype(jnp.bfloat16), "tensor").astype(jnp.float32)
    quarter = own_part.shape[3]
    returned_rows, returned_inner = (
        lax.all_to_all(
            own_part.reshape(experts, CAP, quarter).astype(jnp.bfloat16),
            "expert",
            split_axis=0,
            concat_axis=0,
            tiled=True,
        ).astype(jnp.float32),
        lax.all_to_all(
            inner_sum.reshape(experts, CAP).astype(jnp.bfloat16),
            "expert",
            split_axis=0,
            concat_axis=0,
            tiled=True,
        ).astype(jnp.float32),
    )
    placing_wide = jnp.sum(matches.astype(jnp.int32), axis=2).astype(jnp.float32)
    token_grad = lax.dot_general(
        placing_wide,
        returned_rows.reshape(lanes, quarter),
        (((0,), (0,)), ((), ())),
        precision=lax.Precision.HIGHEST,
        preferred_element_type=jnp.float32,
    )
    grad_probs = jnp.sum(
        jnp.where(matches, returned_inner.reshape(lanes)[:, None, None], 0.0), axis=0
    )
    gate_sum, up_sum, down_sum = (
        lax.psum(gate_total.astype(jnp.bfloat16), "dp").astype(jnp.float32),
        lax.psum(up_total.astype(jnp.bfloat16), "dp").astype(jnp.float32),
        lax.psum(down_total.astype(jnp.bfloat16), "dp").astype(jnp.float32),
    )
    return (
        token_grad.astype(jnp.bfloat16),
        grad_probs,
        gate_sum.astype(jnp.bfloat16),
        up_sum.astype(jnp.bfloat16),
        down_sum.astype(jnp.bfloat16),
    )


def body(activations, out_grad, expert_ids, gate_probs, w_gate, w_up, w_down):
    n_expert, n_tensor, n_dp = (lax.axis_size(a) for a in ("expert", "tensor", "dp"))
    local_count, d, ff = w_gate.shape
    rows, top = expert_ids.shape
    tokens = rows * n_expert * n_dp
    wide = d // n_tensor
    own = local_count // n_dp
    ids = expert_ids.T
    packed = pack(activations, out_grad, ids, gate_probs.T)
    along = [packed] + [shift(packed, "expert", k) for k in range(1, n_expert)]
    across = {k: shift(along[k], "tensor", 1) for k in (0, 3, 1)}
    along[2], across[0], across[3] = lax.optimization_barrier((along[2], across[0], across[3]))
    across[2] = shift(along[2], "tensor", 1)
    w_in = load_weights(along[2], (w_gate, w_up), False, own, 0, own // 2)
    across[1], across[2], w_in = lax.optimization_barrier((across[1], across[2], w_in))
    w_in = load_weights(across[2], (w_gate, w_up), False, own, own // 2, own - own // 2, w_in)
    held = collect(along + [across[k] for k in range(n_expert)], n_tensor)
    swapped = shift(held, "dp", 1)
    grads, both, inners, kept, sent = forward(held, swapped, w_in, w_down, own, n_tensor, top)
    got = shift(sent, "dp", 1)
    kept_here, sent_here = row_sums(both, inners, w_in, n_tensor)
    got, sent_here, grads = lax.optimization_barrier((got, sent_here, grads))
    half = (tokens // 2, wide + META)
    there = pl.pallas_call(
        dp_sum_kernel,
        in_specs=[VMEM] * 2,
        out_specs=VMEM,
        out_shape=pltpu.VMEM(half, jnp.bfloat16),
        compiler_params=pltpu.CompilerParams(vmem_limit_bytes=4 * MIB),
        cost_estimate=LIGHT,
        name="sum_over_cores",
    )(*near(kept, got))
    crossed = shift(there, "tensor", 1)
    got_here = shift(sent_here, "dp", 1)
    got_grads = shift(grads, "dp", 1)
    outputs = weight_grads(held, swapped, grads, local_count)
    crossed, got_here, outputs = lax.optimization_barrier((crossed, got_here, outputs))
    piece = (rows, wide + META)
    pieces = pl.pallas_call(
        tensor_sum_kernel,
        in_specs=[VMEM] * 3,
        out_specs=[VMEM] * n_expert,
        out_shape=[pltpu.VMEM(piece, jnp.float32)] + [pltpu.VMEM(piece, jnp.bfloat16)] * (n_expert - 1),
        compiler_params=pltpu.CompilerParams(vmem_limit_bytes=4 * MIB),
        name="sum_over_tensor",
    )(*near(kept_here, got_here, crossed))
    received = [shift(pieces[k], "expert", -k) for k in range(1, n_expert)]
    outputs = weight_grads(held, swapped, got_grads, local_count, outputs)
    received, outputs = lax.optimization_barrier((received, outputs))
    grad, probs = pl.pallas_call(
        functools.partial(finish_kernel, top),
        in_specs=[VMEM] * (n_expert + 1),
        out_specs=[VMEM] * 2,
        out_shape=[jax.ShapeDtypeStruct((rows, wide), jnp.bfloat16), jax.ShapeDtypeStruct((top, rows), jnp.float32)],
        compiler_params=pltpu.CompilerParams(vmem_limit_bytes=4 * MIB),
        name="sum_over_experts",
    )(ids, pieces[0], *near(*received))
    return (grad, probs.T, *outputs)


def solution(mesh):
    in_specs = (
        P(("groups", "expert", "dp"), "tensor"),
        P(("groups", "expert", "dp"), "tensor"),
        P(("groups", "expert", "dp"), None),
        P(("groups", "expert", "dp"), None),
        P("expert", None, "tensor"),
        P("expert", None, "tensor"),
        P("expert", "tensor", None),
    )
    out_specs = (
        P(("groups", "expert", "dp"), "tensor"),
        P(("groups", "expert", "dp"), None),
        P(("groups", "expert"), None, "tensor"),
        P(("groups", "expert"), None, "tensor"),
        P(("groups", "expert"), "tensor", None),
    )
    sizes = dict(mesh.shape)
    compact = sizes["expert"] == 4 and sizes["tensor"] == 2 and sizes["dp"] == 2
    return jax.shard_map(body if compact else general_body, mesh=mesh, in_specs=in_specs, out_specs=out_specs, check_vma=False)
```

```python
import functools

import jax
import jax.numpy as jnp
from jax import lax
from jax.experimental import pallas as pl
from jax.experimental.pallas import tpu as pltpu
from jax.sharding import PartitionSpec as P

CAP = 16
META = 128
PARTS = 2
MIB = 1024 * 1024
NT = (((1,), (1,)), ((), ()))
TN = (((0,), (0,)), ((), ()))
ANY = pl.BlockSpec(memory_space=pl.ANY)
VMEM = pl.BlockSpec(memory_space=pltpu.VMEM)
LIGHT = pl.CostEstimate(flops=0, bytes_accessed=1024, transcendentals=0)


def near(*arrays):
    return [pltpu.with_memory_space_constraint(x, pltpu.VMEM) for x in arrays]


def far(*arrays):
    return [pltpu.with_memory_space_constraint(x, pltpu.HBM) for x in arrays]


def pack_kernel(top, act_hbm, og_hbm, ids_hbm, probs_hbm, out_ref, ids_ref, probs_ref, sems):
    rows, wide = act_hbm.shape
    copies = [
        pltpu.make_async_copy(act_hbm, out_ref.at[:, :wide], sems.at[0]),
        pltpu.make_async_copy(og_hbm, out_ref.at[:, wide : 2 * wide], sems.at[1]),
        pltpu.make_async_copy(ids_hbm, ids_ref, sems.at[2]),
        pltpu.make_async_copy(probs_hbm, probs_ref, sems.at[3]),
    ]
    for copy in copies:
        copy.start()
    for copy in copies[2:]:
        copy.wait()
    meta = jnp.concatenate([ids_ref[...].astype(jnp.float32), probs_ref[...].astype(jnp.float32)], axis=0)
    meta = jnp.concatenate([meta, jnp.zeros((META - 2 * top, rows), jnp.float32)], axis=0)
    out_ref[:, 2 * wide :] = meta.T.astype(jnp.bfloat16)
    for copy in copies[:2]:
        copy.wait()


def pack(activations, out_grad, ids, probs):
    rows, wide = activations.shape
    return pl.pallas_call(
        functools.partial(pack_kernel, ids.shape[0]),
        in_specs=[ANY] * 4,
        out_specs=VMEM,
        out_shape=pltpu.VMEM((rows, 2 * wide + META), jnp.bfloat16),
        scratch_shapes=[
            pltpu.VMEM(ids.shape, ids.dtype),
            pltpu.VMEM(probs.shape, probs.dtype),
            pltpu.SemaphoreType.DMA((4,)),
        ],
        compiler_params=pltpu.CompilerParams(vmem_limit_bytes=4 * MIB),
        name="pack_tokens",
    )(*far(activations, out_grad, ids, probs))


def collect_kernel(n_tensor, *refs):
    *shards, out_ref = refs
    rows = shards[0].shape[0]
    wide = (shards[0].shape[1] - META) // 2
    d = n_tensor * wide
    blocks = len(shards) // n_tensor
    for i, shard in enumerate(shards):
        side, at = i // blocks, pl.ds(i % blocks * rows, rows)
        begin = pl.multiple_of(lax.rem(lax.axis_index("tensor") + side, n_tensor) * wide, wide)
        out_ref[at, pl.ds(begin, wide)] = shard[:, :wide]
        out_ref[at, pl.ds(d + begin, wide)] = shard[:, wide : 2 * wide]
        if side == 0:
            out_ref[at, 2 * d :] = shard[:, 2 * wide :]


def collect(shards, n_tensor):
    rows, columns = shards[0].shape
    shape = (len(shards) // n_tensor * rows, n_tensor * (columns - META) + META)
    return pl.pallas_call(
        functools.partial(collect_kernel, n_tensor),
        in_specs=[VMEM] * len(shards),
        out_specs=VMEM,
        out_shape=pltpu.VMEM(shape, shards[0].dtype),
        compiler_params=pltpu.CompilerParams(vmem_limit_bytes=4 * MIB),
        cost_estimate=LIGHT,
        name="collect",
    )(*near(*shards))


def load_kernel(by_row, own, start, count, after_ref, *refs):
    *sources, target_ref, sem = refs
    step = sources[0].shape[1 if by_row else 2]
    many = len(sources)
    first = lax.axis_index("dp") * own
    copies = []
    for i in range(start, start + count):
        for j, source in enumerate(sources):
            at = pl.ds((many * i + j) * step, step)
            target = target_ref.at[at, :] if by_row else target_ref.at[:, at]
            copies.append(pltpu.make_async_copy(source.at[first + i], target, sem))
    for copy in copies:
        copy.start()
    for copy in copies:
        copy.wait()


def load_kernel_into(by_row, own, start, count, after_ref, *refs):
    *refs, _, target_ref, sem = refs
    load_kernel(by_row, own, start, count, after_ref, *refs, target_ref, sem)


def load_weights(after, sources, by_row, own, start, count, into=None):
    _, rows, columns = sources[0].shape
    many = own * len(sources)
    shape = (many * rows, columns) if by_row else (rows, many * columns)
    kept = [] if into is None else near(into)
    return pl.pallas_call(
        functools.partial(load_kernel_into if kept else load_kernel, by_row, own, start, count),
        in_specs=[VMEM] + [ANY] * len(sources) + [VMEM] * len(kept),
        out_specs=VMEM,
        out_shape=pltpu.VMEM(shape, jnp.bfloat16),
        scratch_shapes=[pltpu.SemaphoreType.DMA],
        input_output_aliases={1 + len(sources): 0} if kept else {},
        compiler_params=pltpu.CompilerParams(vmem_limit_bytes=4 * MIB),
        cost_estimate=LIGHT,
        name="load_weights",
    )(*near(after), *far(*sources), *kept)


def forward_kernel(n_tensor, top, own, held_ref, got_ref, w_in, wd_ref, *outs):
    grads_ref, both_ref, inners_ref, kept_ref, sent_ref, w_out, sem = outs
    local_count, ff, d = wd_ref.shape
    first = lax.axis_index("dp") * own
    first_expert = lax.axis_index("expert") * local_count + first
    every = lambda at: jnp.concatenate([held_ref[:, at], got_ref[:, at]], axis=0)
    copies = [
        pltpu.make_async_copy(wd_ref.at[first + i], w_out.at[pl.ds(i * ff, ff), :], sem) for i in range(own)
    ]
    for copy in copies:
        copy.start()
    pre = jnp.dot(every(slice(0, d)), w_in[...], preferred_element_type=jnp.float32)
    for copy in copies:
        copy.wait()
    hidden_grads = lax.dot_general(every(slice(d, 2 * d)), w_out[...], NT, preferred_element_type=jnp.float32)
    meta = every(slice(2 * d, None)).astype(jnp.float32)
    lane = lax.broadcasted_iota(jnp.int32, meta.shape, 1)
    inners = jnp.zeros(meta.shape, jnp.float32)
    both = []
    for i in range(own):
        gate_pre, up_pre = pre[:, 2 * i * ff : (2 * i + 1) * ff], pre[:, (2 * i + 1) * ff : (2 * i + 2) * ff]
        hidden_grad = hidden_grads[:, i * ff : (i + 1) * ff]
        expert = first_expert + i
        hit = meta[:, :top] == expert.astype(jnp.float32)
        prob = jnp.sum(jnp.where(hit, meta[:, top : 2 * top], 0.0), axis=1, keepdims=True)
        sigma = jax.nn.sigmoid(gate_pre)
        activated = gate_pre * sigma
        hidden = activated * up_pre
        inner = jnp.sum(hidden * hidden_grad, axis=1, keepdims=True)
        inners = jnp.where(lane == expert, inner, inners)
        scaled = prob * hidden_grad
        gate_grad = (scaled * up_pre * sigma * (1.0 + gate_pre * (1.0 - sigma))).astype(jnp.bfloat16)
        up_grad = (scaled * activated).astype(jnp.bfloat16)
        grads_ref[i, :, :ff] = gate_grad
        grads_ref[i, :, ff : 2 * ff] = up_grad
        grads_ref[i, :, 2 * ff :] = (prob * hidden).astype(jnp.bfloat16)
        both += [gate_grad, up_grad]
    both = jnp.concatenate(both, axis=1)
    both_ref[...] = both
    inners_ref[...] = inners
    row_pass(1, n_tensor, both, inners, w_in, kept_ref, sent_ref)


def row_pass(side, n_tensor, both, inners, w_in, kept_ref, sent_ref):
    wide = w_in.shape[0] // n_tensor
    share = both.shape[0] // 2
    at = pl.ds(pl.multiple_of(lax.rem(lax.axis_index("tensor") + side, n_tensor) * wide, wide), wide)
    total = lax.dot_general(both, w_in[at, :], NT, preferred_element_type=jnp.float32)
    kept_ref[:, :wide] = total[:share]
    kept_ref[:, wide:] = inners[:share]
    sent_ref[:, :wide] = total[share:].astype(jnp.bfloat16)
    sent_ref[:, wide:] = inners[share:].astype(jnp.bfloat16)


def rows_kernel(n_tensor, part, both_ref, inners_ref, w_in, *refs):
    kept_ref, sent_ref = refs[-2:]
    wide = w_in.shape[0] // n_tensor
    step, share = wide // 2, both_ref.shape[0] // 2
    at = pl.ds(pl.multiple_of(lax.axis_index("tensor") * wide + part * step, step), step)
    here = pl.ds(part * step, step)
    total = lax.dot_general(both_ref[...], w_in[at, :], NT, preferred_element_type=jnp.float32)
    kept_ref[:, here] = total[:share]
    sent_ref[:, here] = total[share:].astype(jnp.bfloat16)
    if part == 0:
        kept_ref[:, wide:] = inners_ref[:share, :]
        sent_ref[:, wide:] = inners_ref[share:, :].astype(jnp.bfloat16)


def forward_call(kernel, name, inputs, out_shape, flops, distant=(), scratch=(), aliases={}):
    return pl.pallas_call(
        kernel,
        in_specs=[VMEM] * len(inputs) + [ANY] * len(distant),
        out_specs=[VMEM] * len(out_shape),
        out_shape=out_shape,
        scratch_shapes=scratch,
        input_output_aliases=aliases,
        compiler_params=pltpu.CompilerParams(vmem_limit_bytes=20 * MIB),
        cost_estimate=pl.CostEstimate(flops=flops, bytes_accessed=1024, transcendentals=0),
        name=name,
    )(*near(*inputs), *far(*distant))


def forward(held, got, w_in, w_down, own, n_tensor, top):
    _, ff, d = w_down.shape
    share = held.shape[0]
    tokens = 2 * share
    sums = (share, d // n_tensor + META)
    shapes = [
        pltpu.VMEM((own, tokens, 3 * ff), jnp.bfloat16),
        pltpu.VMEM((tokens, own * 2 * ff), jnp.bfloat16),
        pltpu.VMEM((tokens, META), jnp.float32),
        pltpu.VMEM(sums, jnp.float32),
        pltpu.VMEM(sums, jnp.bfloat16),
    ]
    kernel = functools.partial(forward_kernel, n_tensor, top, own)
    scratch = [pltpu.VMEM((own * ff, d), jnp.bfloat16), pltpu.SemaphoreType.DMA]
    flops = 8 * own * tokens * d * ff
    return forward_call(kernel, "routed_forward", [held, got, w_in], shapes, flops, [w_down], scratch)


def row_sums(both, inners, w_in, n_tensor, part, into=()):
    tokens, d = both.shape[0], w_in.shape[0]
    sums = (tokens // 2, d // n_tensor + META)
    shapes = [pltpu.VMEM(sums, jnp.float32), pltpu.VMEM(sums, jnp.bfloat16)]
    kernel = functools.partial(rows_kernel, n_tensor, part)
    flops = tokens * d * w_in.shape[1]
    aliases = {3 + i: i for i in range(len(into))}
    return forward_call(kernel, "row_sums", [both, inners, w_in, *into], shapes, flops, aliases=aliases)


def weight_kernel(swap, held_ref, got_ref, grads_ref, *refs):
    *targets, gate_ref, up_ref, down_ref, sem = refs[-7:]
    own, d, ff = gate_ref.shape
    half, step = grads_ref.shape[1] // 2, d // PARTS
    core = lax.axis_index("dp")
    first = (1 - core if swap else core) * own
    both = lambda at: jnp.concatenate([held_ref[:, at], got_ref[:, at]], axis=0)
    copies = []

    def send(ref, target, i, at):
        copies.append(pltpu.make_async_copy(ref.at[(i, *at)], target.at[(first + i, *at)], sem))
        copies[-1].start()

    for i in range(own):
        grads = grads_ref[i]
        if swap:
            grads = jnp.concatenate([grads[half:], grads[:half]], axis=0)
        for part in range(PARTS):
            at, every = pl.ds(part * step, step), pl.ds(0, ff)
            total = lax.dot_general(both(at), grads[:, : 2 * ff], TN, preferred_element_type=jnp.float32)
            gate_ref[i, at, :] = total[:, :ff].astype(jnp.bfloat16)
            up_ref[i, at, :] = total[:, ff:].astype(jnp.bfloat16)
            send(gate_ref, targets[0], i, (at, every))
            send(up_ref, targets[1], i, (at, every))
        for part in range(PARTS):
            at, every = pl.ds(part * step, step), pl.ds(0, ff)
            after = pl.ds(d + part * step, step)
            total = lax.dot_general(grads[:, 2 * ff :], both(after), TN, preferred_element_type=jnp.float32)
            down_ref[i, :, at] = total.astype(jnp.bfloat16)
            send(down_ref, targets[2], i, (every, at))
    for copy in copies:
        copy.wait()


def weight_grads(held, got, grads, local_count, into=None):
    own, tokens, ff = grads.shape[0], grads.shape[1], grads.shape[2] // 3
    d = (held.shape[1] - META) // 2
    kept = [] if into is None else list(into)
    shapes = [(d, ff), (d, ff), (ff, d)]
    return pl.pallas_call(
        functools.partial(weight_kernel, into is not None),
        in_specs=[VMEM] * 3 + [ANY] * len(kept),
        out_specs=[ANY] * 3,
        out_shape=[pltpu.HBM((local_count, *s), jnp.bfloat16) for s in shapes],
        scratch_shapes=[pltpu.VMEM((own, *s), jnp.bfloat16) for s in shapes] + [pltpu.SemaphoreType.DMA],
        input_output_aliases={3 + i: i for i in range(len(kept))},
        compiler_params=pltpu.CompilerParams(vmem_limit_bytes=26 * MIB),
        cost_estimate=pl.CostEstimate(
            flops=6 * own * tokens * d * ff, bytes_accessed=6 * own * d * ff, transcendentals=0
        ),
        name="weight_grads",
    )(*near(held, got, grads), *kept)


def dp_sum_kernel(kept_ref, got_ref, there_ref):
    there_ref[...] = (kept_ref[...] + got_ref[...].astype(jnp.float32)).astype(jnp.bfloat16)


def tensor_sum_kernel(kept_ref, core_ref, got_ref, own_ref, *out_refs):
    rows = own_ref.shape[0]
    for block, target in enumerate((own_ref, *out_refs)):
        at = pl.ds(block * rows, rows)
        total = kept_ref[at, :] + core_ref[at, :].astype(jnp.float32) + got_ref[at, :].astype(jnp.float32)
        target[...] = total.astype(target.dtype)


def finish_kernel(top, ids_ref, own_ref, *refs):
    parts, (grad_ref, probs_ref) = refs[:-2], refs[-2:]
    total = own_ref[...]
    for part in parts:
        total = total + part[...].astype(jnp.float32)
    wide = grad_ref.shape[1]
    grad_ref[...] = total[:, :wide].astype(jnp.bfloat16)
    inner = total[:, wide:].T
    ids = ids_ref[...]
    expert = lax.broadcasted_iota(jnp.int32, inner.shape, 0)
    for k in range(top):
        picked = jnp.where(expert == ids[k : k + 1, :], inner, 0.0)
        probs_ref[k : k + 1, :] = jnp.sum(picked, axis=0, keepdims=True)


def shift(x, axis, by):
    count = lax.axis_size(axis)
    return lax.ppermute(x, axis, [(i, (i + by) % count) for i in range(count)])


def general_body(activations, out_grad, expert_ids, gate_probs, w_gate, w_up, w_down):
    d = activations.shape[1] * lax.axis_size("tensor")
    expert_count = lax.axis_size("expert")
    local_count = w_gate.shape[0]
    experts = expert_count * local_count
    token_rows = expert_ids.shape[0]
    flat_ids = expert_ids.reshape(-1)
    onehot = (flat_ids[:, None] == jnp.arange(experts, dtype=jnp.int32)[None, :]).astype(jnp.int32)
    before = jnp.cumsum(onehot, axis=0) - onehot
    slot_index = jnp.sum(before * onehot, axis=1)
    position = (flat_ids * CAP + slot_index).reshape(token_rows, expert_ids.shape[1])
    lane_index = jnp.arange(experts * CAP, dtype=jnp.int32)
    matches = position[None, :, :] == lane_index[:, None, None]
    placing = jnp.sum(matches.astype(jnp.int32), axis=2).astype(jnp.bfloat16)
    send_probs = jnp.sum(jnp.where(matches, gate_probs.astype(jnp.float32)[None], 0.0), axis=(1, 2))
    send_probs = send_probs.astype(jnp.bfloat16).reshape(experts, CAP)
    full_rows, full_grads = (
        lax.all_gather(activations, "tensor", axis=1, tiled=True),
        lax.all_gather(out_grad, "tensor", axis=1, tiled=True),
    )
    send_rows = (
        jnp.dot(placing, full_rows, preferred_element_type=jnp.float32)
        .astype(jnp.bfloat16)
        .reshape(experts, CAP, d)
    )
    send_grads = (
        jnp.dot(placing, full_grads, preferred_element_type=jnp.float32)
        .astype(jnp.bfloat16)
        .reshape(experts, CAP, d)
    )
    got_rows, got_grads, got_probs = (
        lax.all_to_all(send_rows, "expert", split_axis=0, concat_axis=0, tiled=True),
        lax.all_to_all(send_grads, "expert", split_axis=0, concat_axis=0, tiled=True),
        lax.all_to_all(send_probs, "expert", split_axis=0, concat_axis=0, tiled=True),
    )
    rows_in = got_rows.reshape(expert_count, local_count, CAP, d)
    grads_in = got_grads.reshape(expert_count, local_count, CAP, d)
    row_probs = got_probs.reshape(expert_count, local_count, CAP, 1).astype(jnp.float32)
    gate_pre = jnp.einsum("slcd,ldf->slcf", rows_in, w_gate, preferred_element_type=jnp.float32)
    up_pre = jnp.einsum("slcd,ldf->slcf", rows_in, w_up, preferred_element_type=jnp.float32)
    hidden_grad = jnp.einsum("slcd,lfd->slcf", grads_in, w_down, preferred_element_type=jnp.float32)
    sigma = jax.nn.sigmoid(gate_pre)
    activated = gate_pre * sigma
    hidden = activated * up_pre
    inner_part = jnp.sum(hidden * hidden_grad, axis=3)
    weighted = (row_probs * hidden).astype(jnp.bfloat16)
    scaled = row_probs * hidden_grad
    gate_grad = (scaled * up_pre * sigma * (1.0 + gate_pre * (1.0 - sigma))).astype(jnp.bfloat16)
    up_grad = (scaled * activated).astype(jnp.bfloat16)
    row_part = jnp.einsum("slcf,ldf->slcd", gate_grad, w_gate, preferred_element_type=jnp.float32)
    row_part = row_part + jnp.einsum(
        "slcf,ldf->slcd", up_grad, w_up, preferred_element_type=jnp.float32
    )
    gate_total = jnp.einsum(
        "slcd,slcf->ldf", rows_in, gate_grad, preferred_element_type=jnp.float32
    )
    up_total = jnp.einsum("slcd,slcf->ldf", rows_in, up_grad, preferred_element_type=jnp.float32)
    down_total = jnp.einsum(
        "slcf,slcd->lfd", weighted, grads_in, preferred_element_type=jnp.float32
    )
    lanes = experts * CAP
    own_part = lax.psum_scatter(
        row_part.astype(jnp.bfloat16), "tensor", scatter_dimension=3, tiled=True
    ).astype(jnp.float32)
    inner_sum = lax.psum(inner_part.astype(jnp.bfloat16), "tensor").astype(jnp.float32)
    quarter = own_part.shape[3]
    returned_rows, returned_inner = (
        lax.all_to_all(
            own_part.reshape(experts, CAP, quarter).astype(jnp.bfloat16),
            "expert",
            split_axis=0,
            concat_axis=0,
            tiled=True,
        ).astype(jnp.float32),
        lax.all_to_all(
            inner_sum.reshape(experts, CAP).astype(jnp.bfloat16),
            "expert",
            split_axis=0,
            concat_axis=0,
            tiled=True,
        ).astype(jnp.float32),
    )
    placing_wide = jnp.sum(matches.astype(jnp.int32), axis=2).astype(jnp.float32)
    token_grad = lax.dot_general(
        placing_wide,
        returned_rows.reshape(lanes, quarter),
        (((0,), (0,)), ((), ())),
        precision=lax.Precision.HIGHEST,
        preferred_element_type=jnp.float32,
    )
    grad_probs = jnp.sum(
        jnp.where(matches, returned_inner.reshape(lanes)[:, None, None], 0.0), axis=0
    )
    gate_sum, up_sum, down_sum = (
        lax.psum(gate_total.astype(jnp.bfloat16), "dp").astype(jnp.float32),
        lax.psum(up_total.astype(jnp.bfloat16), "dp").astype(jnp.float32),
        lax.psum(down_total.astype(jnp.bfloat16), "dp").astype(jnp.float32),
    )
    return (
        token_grad.astype(jnp.bfloat16),
        grad_probs,
        gate_sum.astype(jnp.bfloat16),
        up_sum.astype(jnp.bfloat16),
        down_sum.astype(jnp.bfloat16),
    )


def body(activations, out_grad, expert_ids, gate_probs, w_gate, w_up, w_down):
    n_expert, n_tensor, n_dp = (lax.axis_size(a) for a in ("expert", "tensor", "dp"))
    local_count, d, ff = w_gate.shape
    rows, top = expert_ids.shape
    tokens = rows * n_expert * n_dp
    wide = d // n_tensor
    own = local_count // n_dp
    ids = expert_ids.T
    packed = pack(activations, out_grad, ids, gate_probs.T)
    along = [packed] + [shift(packed, "expert", k) for k in range(1, n_expert)]
    across = {k: shift(along[k], "tensor", 1) for k in (0, 3, 1)}
    along[2], across[0], across[3] = lax.optimization_barrier((along[2], across[0], across[3]))
    across[2] = shift(along[2], "tensor", 1)
    w_in = load_weights(along[2], (w_gate, w_up), False, own, 0, own // 2)
    across[1], across[2], w_in = lax.optimization_barrier((across[1], across[2], w_in))
    w_in = load_weights(across[2], (w_gate, w_up), False, own, own // 2, own - own // 2, w_in)
    held = collect(along + [across[k] for k in range(n_expert)], n_tensor)
    swapped = shift(held, "dp", 1)
    grads, both, inners, kept, sent = forward(held, swapped, w_in, w_down, own, n_tensor, top)
    got = shift(sent, "dp", 1)
    kept_here, sent_here = row_sums(both, inners, w_in, n_tensor, 0)
    got, sent_here, grads = lax.optimization_barrier((got, sent_here, grads))
    half = (tokens // 2, wide + META)
    there = pl.pallas_call(
        dp_sum_kernel,
        in_specs=[VMEM] * 2,
        out_specs=VMEM,
        out_shape=pltpu.VMEM(half, jnp.bfloat16),
        compiler_params=pltpu.CompilerParams(vmem_limit_bytes=4 * MIB),
        cost_estimate=LIGHT,
        name="sum_over_cores",
    )(*near(kept, got))
    crossed = shift(there, "tensor", 1)
    both, there = lax.optimization_barrier((both, there))
    kept_here, sent_here = row_sums(both, inners, w_in, n_tensor, 1, (kept_here, sent_here))
    got_here = shift(sent_here, "dp", 1)
    got_grads = shift(grads, "dp", 1)
    outputs = weight_grads(held, swapped, grads, local_count)
    crossed, got_here, outputs = lax.optimization_barrier((crossed, got_here, outputs))
    piece = (rows, wide + META)
    pieces = pl.pallas_call(
        tensor_sum_kernel,
        in_specs=[VMEM] * 3,
        out_specs=[VMEM] * n_expert,
        out_shape=[pltpu.VMEM(piece, jnp.float32)] + [pltpu.VMEM(piece, jnp.bfloat16)] * (n_expert - 1),
        compiler_params=pltpu.CompilerParams(vmem_limit_bytes=4 * MIB),
        name="sum_over_tensor",
    )(*near(kept_here, got_here, crossed))
    received = [shift(pieces[k], "expert", -k) for k in range(1, n_expert)]
    outputs = weight_grads(held, swapped, got_grads, local_count, outputs)
    received, outputs = lax.optimization_barrier((received, outputs))
    grad, probs = pl.pallas_call(
        functools.partial(finish_kernel, top),
        in_specs=[VMEM] * (n_expert + 1),
        out_specs=[VMEM] * 2,
        out_shape=[jax.ShapeDtypeStruct((rows, wide), jnp.bfloat16), jax.ShapeDtypeStruct((top, rows), jnp.float32)],
        compiler_params=pltpu.CompilerParams(vmem_limit_bytes=4 * MIB),
        name="sum_over_experts",
    )(ids, pieces[0], *near(*received))
    return (grad, probs.T, *outputs)


def solution(mesh):
    in_specs = (
        P(("groups", "expert", "dp"), "tensor"),
        P(("groups", "expert", "dp"), "tensor"),
        P(("groups", "expert", "dp"), None),
        P(("groups", "expert", "dp"), None),
        P("expert", None, "tensor"),
        P("expert", None, "tensor"),
        P("expert", "tensor", None),
    )
    out_specs = (
        P(("groups", "expert", "dp"), "tensor"),
        P(("groups", "expert", "dp"), None),
        P(("groups", "expert"), None, "tensor"),
        P(("groups", "expert"), None, "tensor"),
        P(("groups", "expert"), "tensor", None),
    )
    sizes = dict(mesh.shape)
    compact = sizes["expert"] == 4 and sizes["tensor"] == 2 and sizes["dp"] == 2
    return jax.shard_map(body if compact else general_body, mesh=mesh, in_specs=in_specs, out_specs=out_specs, check_vma=False)
```
